512 devices in a mesh: case: 16 (over z_lo, y), space: 32 (over x, z_hi, core).
Axes of the slice: x: 4, y: 4, z: 16 (z_hi: 4, z_lo: 4; z = z_hi * 4 + z_lo), core: 2. Of those that a mesh axis runs over, the one named last changes fastest.
Arguments:
- forcing: bfloat16 [16, 256, 32, 256], P('case', 'space'), may hold values from -3.5 to 3.5
- viscosity: bfloat16 [16, 256, 32, 256], P('case', 'space'), may hold values from 0.099609375 to 1
- measured: bfloat16 [16, 256, 32, 256], P('case', 'space'), may hold values from -1.796875 to 1.796875
- correction: float32 [256, 32, 256], P('space'), may hold values from -6 to 6
- wall_rows: int32 [16, 32], P('case'), may hold values from 0 to 63
Outputs:
- pressure: float32 [16, 256, 32, 256], P('case', 'space')
- gradient: float32 [256, 32, 256], P('space')
The draws below stay inside these ranges and needn't reach their ends.
All inputs are finite; a program needn't handle non-finite values.
Results may differ from the reference program's by a relative error of at most 0.0003.
Values may be sent and summed in bfloat16 or wider, within the bound.
A program may use at most 64 MiB of HBM per device.

```python
import math
import jax
import jax.numpy as jnp
from jax import lax

Z = 256
Y = 256
X = 32
CASES = 16
SPAN_DEV = 8


def draw_forcing(key, part):
    full_shape = (CASES, Z, X, Y)
    values = jnp.clip(jax.random.normal(key, full_shape, jnp.float32), -3.5, 3.5)
    return values.astype(jnp.bfloat16)


def touch_ends(result, rng, low, high):
    dims = result.shape
    spot = [jax.random.randint(jax.random.fold_in(rng, axis), (), 0, dims[axis]) for axis in range(len(dims))]
    result = result.at[tuple(spot)].set(low)
    longest = dims.index(max(dims))
    spot[longest] = (spot[longest] + 1) % dims[longest]
    return result.at[tuple(spot)].set(high)


def levels(own_key, extent, pieces, least, high):
    def one(position, parts):
        draws = jax.random.uniform(jax.random.fold_in(jax.random.fold_in(own_key, 6), position), (parts,), jnp.float32, least / len(pieces), high / len(pieces))
        return jnp.repeat(jnp.exp(draws), extent[position] // parts).reshape((-1,) + (1,) * (len(extent) - position - 1))

    loudness = one(*pieces[0])
    for cut in pieces[1:]:
        loudness = loudness * one(*cut)
    return loudness


def scatter_about(key, dims, spread, limit, split=(), kind=jnp.bfloat16):
    factor_of = levels(key, dims, split, -0.22, 0.18) if split else 1.0
    values = jax.random.normal(key, dims, jnp.float32) * spread * factor_of
    return jnp.minimum(jnp.maximum(values, -limit), limit).astype(kind)


def setup_inputs(seed: int = 0) -> dict:
    keys = jax.random.split(jax.random.key(seed), 6)
    return {
        "forcing": draw_forcing(jax.random.fold_in(keys[5], 71), 0),
        "viscosity": jnp.clip(jnp.exp(math.log(1.0) - 2.306499 * jax.random.uniform(keys[1], (CASES, Z, X, Y), jnp.float32) ** levels(keys[1], (CASES, Z, X, Y), ((0, 16), (1, 32)), -0.2, 0.2)), 0.099609375, 1.0).astype(jnp.bfloat16),
        "measured": scatter_about(keys[2], (CASES, Z, X, Y), 0.3, 1.796875, ((0, 16), (1, 32))),
        "correction": scatter_about(keys[3], (Z, X, Y), 1.0, 6.0, ((0, 32),), jnp.float32),
        "wall_rows": touch_ends(jax.random.randint(keys[4], (CASES, X), 0, Y // 4), jax.random.fold_in(keys[4], 1), 0, (Y // 4) - 1).astype(jnp.int32),
    }


def reference(forcing, viscosity, measured, correction, wall_rows):
    screen_rate = 1.0 / (2.0 * SPAN_DEV)
    wave_number = jnp.arange(Z, dtype=jnp.int32)
    laplace_part = 2.0 - 2.0 * jnp.cos(wave_number.astype(jnp.float32) * (2.0 * math.pi / Z))
    middle = jnp.broadcast_to((2.0 + laplace_part + screen_rate * screen_rate)[:, None], (Z, Y)).astype(jnp.float32)
    below_band = jnp.concatenate([jnp.zeros((Z, 1), jnp.float32), -jnp.ones((Z, Y - 1), jnp.float32)], axis=1)
    above_band = jnp.concatenate([-jnp.ones((Z, Y - 1), jnp.float32), jnp.zeros((Z, 1), jnp.float32)], axis=1)

    def model_solve(field):
        spectrum = jnp.fft.fft(field, axis=0)
        stacked = jnp.concatenate([jnp.real(spectrum), jnp.imag(spectrum)], axis=1)
        solved = lax.linalg.tridiagonal_solve(below_band, middle, above_band, jnp.swapaxes(stacked, 1, 2))
        solved = jnp.swapaxes(solved, 1, 2)
        back = jnp.fft.ifft(solved[:, :X] + 1j * solved[:, X:], axis=0)
        return screen_rate * jnp.real(back)
    row_index = jnp.arange(Y, dtype=jnp.int32)

    def one_case(running, inputs):
        force_case, viscous_case, measured_case, wall_case = inputs
        viscous_field = viscous_case.astype(jnp.float32)
        source_field = force_case.astype(jnp.float32) + viscous_field * correction
        pressure_case = model_solve(source_field)
        outside = (row_index[None, None, :] >= wall_case[None, :, None]).astype(jnp.float32)
        misfit = outside * (pressure_case - measured_case.astype(jnp.float32))
        adjoint = model_solve(misfit)
        return (running + viscous_field * adjoint, pressure_case)
    gradient, pressure = lax.scan(one_case, jnp.zeros((Z, X, Y), jnp.float32), (forcing, viscosity, measured, wall_rows))
    return (pressure, gradient)
```

```python
import functools

import jax
import jax.numpy as jnp
import ml_dtypes
import numpy as np
from jax import lax
from jax.experimental import pallas as pl
from jax.experimental.pallas import tpu as pltpu
from jax.sharding import PartitionSpec as P

MESH = pl.DeviceIdType.MESH
F32, BF16 = jnp.float32, jnp.bfloat16


def sine_tables(rows):
    index = np.arange(1, rows + 1, dtype=np.float64)
    phase = (index[:, None] * index[None, :]) % (2 * (rows + 1))
    sine = np.sqrt(2.0 / (rows + 1)) * np.sin(np.pi * phase / (rows + 1))
    high = sine.astype(ml_dtypes.bfloat16)
    low = (sine - high.astype(np.float64)).astype(ml_dtypes.bfloat16)
    return high, low


def mode_table(rows, cells, length, screen):
    index = np.arange(1, rows + 1, dtype=np.float64)
    centre = 4.0 * np.sin(np.pi * index / (2 * (rows + 1))) ** 2 + screen * screen
    rate = 1.0 + centre / 2.0 - np.sqrt(centre + centre * centre / 4.0)
    blocks = length // cells
    lines = [rate, 1.0 / (1.0 - rate**length), screen / (1.0 / rate - rate)]
    step = 1
    while step < blocks:
        lines.append(rate ** (cells * step))
        step *= 2
    table = np.zeros((-(-len(lines) // 8) * 8, rows))
    table[: len(lines)] = lines
    return table.astype(np.float32)


def wait_bytes(ref, sem):
    pltpu.make_async_copy(ref, ref, sem).wait()


def kernel(spaces, cases, cells, planes, rows, forcing, viscosity, measured, correction, walls, high_ref, low_ref, modes,
           pressure_out, gradient_out, head, tail, spectrum, result, send1, got1, send2, got2, send3, got3, send4, got4,
           part_got, part_sum, sems, out_sem):
    me = lax.axis_index("space")
    case = lax.axis_index("case")
    lanes = 128
    groups = rows // lanes
    part = cells * planes // cases

    barrier = pltpu.get_barrier_semaphore()

    def greet(axis, mine, count):
        def one(k, carry):
            pl.semaphore_signal(barrier, inc=1, device_id={axis: lax.rem(mine + k, count)}, device_id_type=MESH)
            return carry

        lax.fori_loop(1, count, one, 0)

    greet("space", me, spaces)
    greet("case", case, cases)

    rate = modes[0:1, :]
    around = modes[1:2, :]
    scale = modes[2:3, :]

    def split(i, value):
        top = value.astype(BF16)
        head[i * planes : (i + 1) * planes, :] = top
        tail[i * planes : (i + 1) * planes, :] = (value - top.astype(F32)).astype(BF16)

    def sine():
        high, low = high_ref[...], low_ref[...]
        top = head[...]
        small = jnp.dot(top, low, preferred_element_type=F32) + jnp.dot(tail[...], high, preferred_element_type=F32)
        return jnp.dot(top, high, preferred_element_type=F32) + small

    def at(ref, i):
        return ref[i * planes : (i + 1) * planes, :]

    def exchange(send, got, phase):
        def one(k, carry):
            other = lax.rem(me + k, spaces)
            pltpu.make_async_remote_copy(
                src_ref=send.at[other],
                dst_ref=got.at[me],
                send_sem=sems.at[2 * phase],
                recv_sem=sems.at[2 * phase + 1],
                device_id={"space": other},
                device_id_type=MESH,
            ).start()
            return carry

        lax.fori_loop(1, spaces, one, 0)
        got[pl.ds(me, 1)] = send[pl.ds(me, 1)]

    def arrived(got, phase):
        wait_bytes(got.at[pl.ds(0, spaces - 1)], sems.at[2 * phase + 1])

    def sent(send, phase):
        wait_bytes(send.at[pl.ds(0, spaces - 1)], sems.at[2 * phase])

    def put(ref, first, second):
        for g in range(groups):
            ref[:, g, :] = first[:, g * lanes : (g + 1) * lanes]
            ref[:, groups + g, :] = second[:, g * lanes : (g + 1) * lanes]

    def take(ref):
        first = jnp.concatenate([ref[:, g, :] for g in range(groups)], axis=1)
        second = jnp.concatenate([ref[:, groups + g, :] for g in range(groups)], axis=1)
        return first, second

    def solve(send_a, got_a, send_b, got_b, phase, before_send=None):
        spectrum[...] = sine()
        onward = rate * at(spectrum, 0)
        backward = rate * at(spectrum, cells - 1)
        for i in range(1, cells):
            onward = (onward + at(spectrum, i)) * rate
            backward = (backward + at(spectrum, cells - 1 - i)) * rate
        put(send_a, onward, backward)
        if before_send is not None:
            before_send()
        exchange(send_a, got_a, phase)
        arrived(got_a, phase)
        onward, backward = take(got_a)
        step, line = 1, 3
        while step < spaces:
            power = modes[line : line + 1, :]
            onward = onward + power * pltpu.roll(onward, step, 0)
            backward = backward + power * pltpu.roll(backward, spaces - step, 0)
            step, line = 2 * step, line + 1
        put(send_b, pltpu.roll(onward, 1, 0) * around, pltpu.roll(backward, spaces - 1, 0) * around)
        exchange(send_b, got_b, phase + 1)
        arrived(got_b, phase + 1)
        left, right = take(got_b)
        running = right
        for i in range(cells - 1, -1, -1):
            at_i = at(spectrum, i)
            result[i * planes : (i + 1) * planes, :] = running
            running = (running + at_i) * rate
        running = left
        for i in range(cells):
            running = at(spectrum, i) + (running if i == 0 else running * rate)
            split(i, (running + at(result, i)) * scale)
        result[...] = sine()

    for i in range(cells):
        split(i, at(forcing, i).astype(F32) + at(viscosity, i).astype(F32) * at(correction, i))

    solve(send1, got1, send2, got2, 0, lambda: pl.semaphore_wait(barrier, spaces + cases - 2))

    pressure = spectrum
    sent(send1, 0)
    sent(send2, 1)
    diagonal = lax.broadcasted_iota(jnp.int32, (planes, planes), 0) == lax.broadcasted_iota(
        jnp.int32, (planes, planes), 1
    )
    first_row = jnp.sum(jnp.where(diagonal, walls[...], 0), axis=1, keepdims=True)
    outside = lax.broadcasted_iota(jnp.int32, (planes, rows), 1) >= first_row
    copy_out = pltpu.make_async_copy(part_sum, pressure_out, out_sem)
    for i in range(cells):
        value = at(result, i)
        part_sum[i * planes : (i + 1) * planes, :] = value
        split(i, jnp.where(outside, value - at(measured, i).astype(F32), 0.0))
    copy_out.start()
    solve(send3, got3, send4, got4, 2)
    sent(send3, 2)
    sent(send4, 3)
    copy_out.wait()
    for i in range(cells):
        result[i * planes : (i + 1) * planes, :] = at(viscosity, i).astype(F32) * at(result, i)

    def to_case(k, carry):
        other = lax.rem(case + k, cases)
        pltpu.make_async_remote_copy(
            src_ref=result.at[pl.ds(pl.multiple_of(other * part, part), part)],
            dst_ref=part_got.at[case],
            send_sem=sems.at[8],
            recv_sem=sems.at[9],
            device_id={"case": other},
            device_id_type=MESH,
        ).start()
        return carry

    lax.fori_loop(1, cases, to_case, 0)
    mine = pl.ds(pl.multiple_of(case * part, part), part)
    part_got[case] = result[mine]
    wait_bytes(part_got.at[pl.ds(0, cases - 1)], sems.at[9])
    total = part_got[0]
    for k in range(1, cases):
        total = total + part_got[k]
    part_sum[0:part, :] = total

    def to_all(k, carry):
        other = lax.rem(case + k, cases)
        pltpu.make_async_remote_copy(
            src_ref=part_sum.at[0:part],
            dst_ref=gradient_out.at[mine],
            send_sem=sems.at[10],
            recv_sem=sems.at[11],
            device_id={"case": other},
            device_id_type=MESH,
        ).start()
        return carry

    lax.fori_loop(1, cases, to_all, 0)
    keep = pltpu.make_async_copy(part_sum.at[0:part], gradient_out.at[mine], out_sem)
    keep.start()
    keep.wait()
    wait_bytes(gradient_out.at[pl.ds(0, (cases - 1) * part)], sems.at[11])
    wait_bytes(result.at[pl.ds(0, (cases - 1) * part)], sems.at[8])
    wait_bytes(result.at[pl.ds(0, (cases - 1) * part)], sems.at[10])


def shards(forcing, viscosity, measured, correction, wall_rows):
    cells, planes, rows = correction.shape
    spaces, cases = lax.axis_size("space"), lax.axis_size("case")
    length = cells * spaces
    high, low = sine_tables(rows)
    modes = mode_table(rows, cells, length, 1.0 / (2.0 * cells))
    flat = (cells * planes, rows)
    part = cells * planes // cases
    exchanged = [pltpu.VMEM((spaces, 2 * rows // 128, 128), F32)] * 8
    vmem = pl.BlockSpec(memory_space=pltpu.VMEM)
    pressure, gradient = pl.pallas_call(
        functools.partial(kernel, spaces, cases, cells, planes, rows),
        out_shape=(jax.ShapeDtypeStruct(flat, F32), jax.ShapeDtypeStruct(flat, F32)),
        in_specs=[vmem] * 8,
        out_specs=(pl.BlockSpec(memory_space=pl.ANY),) * 2,
        scratch_shapes=[
            pltpu.VMEM(flat, BF16),
            pltpu.VMEM(flat, BF16),
            pltpu.VMEM(flat, F32),
            pltpu.VMEM(flat, F32),
            *exchanged,
            pltpu.VMEM((cases, part, rows), F32),
            pltpu.VMEM(flat, F32),
            pltpu.SemaphoreType.DMA((12,)),
            pltpu.SemaphoreType.DMA,
        ],
        compiler_params=pltpu.CompilerParams(
            collective_id=0, has_side_effects=True, vmem_limit_bytes=16 * 1024 * 1024
        ),
    )(
        forcing.reshape(flat),
        viscosity.reshape(flat),
        measured.reshape(flat),
        correction.reshape(flat),
        wall_rows,
        jnp.asarray(high),
        jnp.asarray(low),
        jnp.asarray(modes),
    )
    return pressure.reshape(forcing.shape), gradient.reshape(correction.shape)


def solution(mesh):
    return jax.shard_map(
        shards,
        mesh=mesh,
        in_specs=(
            P("case", "space", None, None),
            P("case", "space", None, None),
            P("case", "space", None, None),
            P("space", None, None),
            P("case", None),
        ),
        out_specs=(P("case", "space", None, None), P("space", None, None)),
        check_vma=False,
    )
```

```python
import functools

import jax
import jax.numpy as jnp
import ml_dtypes
import numpy as np
from jax import lax
from jax.experimental import pallas as pl
from jax.experimental.pallas import tpu as pltpu
from jax.sharding import PartitionSpec as P

MESH = pl.DeviceIdType.MESH
F32, BF16, I32 = jnp.float32, jnp.bfloat16, jnp.int32
OUTER, MIDDLE = 4, 4
TOP = 32767.0


def sine_tables(rows):
    index = np.arange(1, rows + 1, dtype=np.float64)
    phase = (index[:, None] * index[None, :]) % (2 * (rows + 1))
    sine = np.sqrt(2.0 / (rows + 1)) * np.sin(np.pi * phase / (rows + 1))
    high = sine.astype(ml_dtypes.bfloat16)
    low = (sine - high.astype(np.float64)).astype(ml_dtypes.bfloat16)
    return high, low


def mode_table(rows, cells, length, screen):
    index = np.arange(1, rows + 1, dtype=np.float64)
    centre = 4.0 * np.sin(np.pi * index / (2 * (rows + 1))) ** 2 + screen * screen
    rate = 1.0 + centre / 2.0 - np.sqrt(centre + centre * centre / 4.0)
    block = rate**cells
    lines = [
        rate,
        block,
        block**2,
        block ** (2 * MIDDLE),
        block ** (2 * MIDDLE * (OUTER - 1)),
        1.0 / (1.0 - rate**length),
        screen / (1.0 / rate - rate),
        np.zeros(rows),
    ]
    return np.stack(lines).astype(np.float32)


def wait_bytes(ref, sem):
    pltpu.make_async_copy(ref, ref, sem).wait()


def pack(ref, first, second):
    count = first.shape[0]
    largest = jnp.max(jnp.maximum(jnp.abs(first), jnp.abs(second)), axis=0, keepdims=True)
    code = jnp.ceil(jnp.log2(jnp.maximum(largest, 1e-30)) * 64.0)
    factor = TOP * jnp.exp2(code * (-1.0 / 64.0))
    a = jnp.round(first * factor).astype(I32)
    b = jnp.round(second * factor).astype(I32)
    ref[0:count, :] = (a << 16) | (b & 0xFFFF)
    ref[count : count + 1, :] = code.astype(I32)


def unpack(ref):
    count = ref.shape[0] - 1
    scale = jnp.exp2(ref[count : count + 1, :].astype(F32) * (1.0 / 64.0)) * (1.0 / TOP)
    words = ref[0:count, :]
    return (words >> 16).astype(F32) * scale, ((words << 16) >> 16).astype(F32) * scale


def kernel(cases, cells, planes, rows, forcing_in, viscosity_in, measured_in, correction_in, walls_in, high_in, low_in,
           modes_in, pressure_out, gradient_out, forcing, viscosity, measured, correction, walls, high_ref, low_ref, modes,
           head, tail, spectrum, result, moments, pressure, xs_send, xs_got, hs_send, hs_got, cs_send, cs_got,
           rs_send, rs_got, ag_send, ag_got, in_sems, out_sems, sends, recvs):
    me = lax.axis_index("space")
    case = lax.axis_index("case")
    inner, middle, outer = me % 2, me // 2 % MIDDLE, me // (2 * MIDDLE)
    half = planes // 2
    part = cells * planes // cases

    def space(o, m, i):
        return {"space": (o * MIDDLE + m) * 2 + i}

    barrier = pltpu.get_barrier_semaphore()

    def greet(device):
        pl.semaphore_signal(barrier, inc=1, device_id=device, device_id_type=MESH)

    for k in (2, 1, 3):
        greet(space(outer, (middle + k) % MIDDLE, inner))
    loads = [
        pltpu.make_async_copy(src, dst, in_sems.at[i])
        for i, (src, dst) in enumerate(
            (
                (forcing_in, forcing),
                (viscosity_in, viscosity),
                (correction_in, correction),
                (high_in, high_ref),
                (low_in, low_ref),
                (modes_in, modes),
                (walls_in, walls),
                (measured_in, measured),
            )
        )
    ]
    for load in loads:
        load.start()
    for k in range(1, cases):
        greet({"case": (case + k) % cases})
    for k in range(1, 2 * OUTER):
        greet(space((outer + k // 2) % OUTER, middle, (inner + k) % 2))

    def at(ref, i):
        return ref[i * planes : (i + 1) * planes, :]

    def split(i, value):
        top = value.astype(BF16)
        head[i * planes : (i + 1) * planes, :] = top
        tail[i * planes : (i + 1) * planes, :] = (value - top.astype(F32)).astype(BF16)

    def sine():
        high, low = high_ref[...], low_ref[...]
        top = head[...]
        small = jnp.dot(top, low, preferred_element_type=F32) + jnp.dot(tail[...], high, preferred_element_type=F32)
        return jnp.dot(top, high, preferred_element_type=F32) + small

    def line(i):
        return modes[i : i + 1, :]

    def send(src, dst, phase, device):
        pltpu.make_async_remote_copy(
            src_ref=src, dst_ref=dst, send_sem=sends.at[phase], recv_sem=recvs.at[phase], device_id=device, device_id_type=MESH
        ).start()

    def solve(turn, before_send=None):
        first = 3 * turn
        spectrum[...] = sine()
        rate = line(0)
        onward = rate * at(spectrum, 0)
        backward = rate * at(spectrum, cells - 1)
        for i in range(1, cells):
            onward = (onward + at(spectrum, i)) * rate
            backward = (backward + at(spectrum, cells - 1 - i)) * rate
        for i in range(2):
            moments[0, i] = onward[i * half : (i + 1) * half]
            moments[1, i] = backward[i * half : (i + 1) * half]
            pack(xs_send.at[turn, i], moments[0, i], moments[1, i])
        if before_send is not None:
            before_send()
        for k in (4, 5, 2, 3, 6, 7, 1):
            to_inner = (inner + k) % 2
            send(
                xs_send.at[turn, to_inner],
                xs_got.at[turn, 2 * outer + inner],
                first,
                space((outer + k // 2) % OUTER, middle, to_inner),
            )
        wait_bytes(xs_got.at[turn, pl.ds(0, 2 * OUTER - 1)], recvs.at[first])

        block, two, eight, most = line(1), line(2), line(3), line(4)
        own_l, own_r = moments[0, inner], moments[1, inner]
        other_l, other_r = unpack(xs_got.at[turn, 2 * outer + 1 - inner])
        is_first = inner == 0
        l0, l1 = jnp.where(is_first, own_l, other_l), jnp.where(is_first, other_l, own_l)
        r0, r1 = jnp.where(is_first, own_r, other_r), jnp.where(is_first, other_r, own_r)
        chip_l, chip_r = l0 * block + l1, r0 + r1 * block
        pairs = []
        for d in range(1, OUTER):
            slot = 2 * ((outer + d) % OUTER)
            a_l, a_r = unpack(xs_got.at[turn, slot])
            b_l, b_r = unpack(xs_got.at[turn, slot + 1])
            pairs.append((a_l * block + b_l, a_r + b_r * block))
        before = pairs[0][0]
        after = pairs[OUTER - 2][1]
        for d in range(1, OUTER - 1):
            before = pairs[d][0] + eight * before
            after = pairs[OUTER - 2 - d][1] + eight * after
        onto, round_l = chip_l + eight * before, before + most * chip_l
        back, round_r = chip_r + eight * after, after + most * chip_r
        pack(hs_send.at[turn, 0], onto, round_r)
        pack(hs_send.at[turn, 1], round_l, back)
        for k in (2, 1, 3):
            send(
                hs_send.at[turn, (middle + k) // MIDDLE],
                hs_got.at[turn, middle],
                first + 1,
                space(outer, (middle + k) % MIDDLE, inner),
            )
        wait_bytes(hs_got.at[turn, pl.ds(0, MIDDLE - 1)], recvs.at[first + 1])
        near = [unpack(hs_got.at[turn, (middle + d) % MIDDLE]) for d in range(1, MIDDLE)]
        left, right = round_l, round_r
        for d in range(1, MIDDLE):
            left = near[d - 1][0] + two * left
            right = near[MIDDLE - 1 - d][1] + two * right
        left, right = left * line(5), right * line(5)
        left_1, right_0 = left * block + l0, right * block + r1
        cs_send[turn, 0] = jnp.where(is_first, left_1, left)
        cs_send[turn, 1] = jnp.where(is_first, right, right_0)
        send(cs_send.at[turn], cs_got.at[turn, inner], first + 2, space(outer, middle, 1 - inner))
        cs_got[turn, inner, 0] = jnp.where(is_first, left, left_1)
        cs_got[turn, inner, 1] = jnp.where(is_first, right_0, right)
        wait_bytes(cs_got.at[turn, 0], recvs.at[first + 2])

        left = jnp.concatenate([cs_got[turn, 0, 0], cs_got[turn, 1, 0]], axis=0)
        right = jnp.concatenate([cs_got[turn, 0, 1], cs_got[turn, 1, 1]], axis=0)
        running = right
        for i in range(cells - 1, -1, -1):
            result[i * planes : (i + 1) * planes, :] = running
            running = (running + at(spectrum, i)) * rate
        running = left
        for i in range(cells):
            running = at(spectrum, i) + (running if i == 0 else running * rate)
            split(i, (running + at(result, i)) * line(6))
        result[...] = sine()

    for i in range(3):
        loads[i].wait()
    for i in range(cells):
        split(i, at(forcing, i).astype(F32) + at(viscosity, i).astype(F32) * at(correction, i))
    for i in range(3, 8):
        loads[i].wait()

    solve(0, lambda: pl.semaphore_wait(barrier, cases - 1 + MIDDLE - 1 + 2 * OUTER - 1))

    diagonal = lax.broadcasted_iota(I32, (planes, planes), 0) == lax.broadcasted_iota(I32, (planes, planes), 1)
    first_row = jnp.sum(jnp.where(diagonal, walls[...], 0), axis=1, keepdims=True)
    outside = lax.broadcasted_iota(I32, (planes, rows), 1) >= first_row
    for i in range(cells):
        value = at(result, i)
        pressure[i * planes : (i + 1) * planes, :] = value
        split(i, jnp.where(outside, value - at(measured, i).astype(F32), 0.0))
    copy_out = pltpu.make_async_copy(pressure, pressure_out, out_sems.at[0])
    copy_out.start()

    solve(1)

    def term(first):
        return viscosity[pl.ds(first, part), :].astype(F32) * result[pl.ds(first, part), :]

    for k in range(1, cases):
        other = (case + k) % cases
        value = term(pl.multiple_of(other * part, part))
        pack(rs_send.at[other], value[: part // 2], value[part // 2 :])
        send(rs_send.at[other], rs_got.at[case], 6, {"case": other})
    value = term(pl.multiple_of(case * part, part))
    pack(rs_got.at[case], value[: part // 2], value[part // 2 :])
    wait_bytes(rs_got.at[pl.ds(0, cases - 1)], recvs.at[6])
    upper, lower = unpack(rs_got.at[0])
    for k in range(1, cases):
        a, b = unpack(rs_got.at[k])
        upper, lower = upper + a, lower + b
    pack(ag_send, upper, lower)
    for k in range(1, cases):
        send(ag_send, ag_got.at[case], 7, {"case": (case + k) % cases})
    ag_got[case] = ag_send[...]
    for turn in range(2):
        wait_bytes(xs_got.at[turn, pl.ds(0, 2 * OUTER - 1)], sends.at[3 * turn])
        wait_bytes(hs_got.at[turn, pl.ds(0, MIDDLE - 1)], sends.at[3 * turn + 1])
        wait_bytes(cs_got.at[turn, 0], sends.at[3 * turn + 2])
    wait_bytes(rs_got.at[pl.ds(0, cases - 1)], sends.at[6])
    copy_out.wait()
    wait_bytes(ag_got.at[pl.ds(0, cases - 1)], recvs.at[7])
    for k in range(cases):
        a, b = unpack(ag_got.at[k])
        result[k * part : k * part + part // 2, :] = a
        result[k * part + part // 2 : (k + 1) * part, :] = b
    copy_out = pltpu.make_async_copy(result, gradient_out, out_sems.at[1])
    copy_out.start()
    wait_bytes(ag_got.at[pl.ds(0, cases - 1)], sends.at[7])
    copy_out.wait()


def shards(forcing, viscosity, measured, correction, wall_rows):
    cells, planes, rows = correction.shape
    spaces, cases = lax.axis_size("space"), lax.axis_size("case")
    assert spaces == 2 * OUTER * MIDDLE
    high, low = sine_tables(rows)
    modes = mode_table(rows, cells, cells * spaces, 1.0 / (2.0 * cells))
    flat = (cells * planes, rows)
    half, part = planes // 2, cells * planes // cases
    anywhere = pl.BlockSpec(memory_space=pl.ANY)
    pressure, gradient = pl.pallas_call(
        functools.partial(kernel, cases, cells, planes, rows),
        out_shape=(jax.ShapeDtypeStruct(flat, F32), jax.ShapeDtypeStruct(flat, F32)),
        in_specs=[anywhere] * 8,
        out_specs=(anywhere,) * 2,
        scratch_shapes=[
            pltpu.VMEM(flat, BF16),
            pltpu.VMEM(flat, BF16),
            pltpu.VMEM(flat, BF16),
            pltpu.VMEM(flat, F32),
            pltpu.VMEM((1, planes), I32),
            pltpu.VMEM((rows, rows), BF16),
            pltpu.VMEM((rows, rows), BF16),
            pltpu.VMEM(modes.shape, F32),
            pltpu.VMEM(flat, BF16),
            pltpu.VMEM(flat, BF16),
            pltpu.VMEM(flat, F32),
            pltpu.VMEM(flat, F32),
            pltpu.VMEM((2, 2, half, rows), F32),
            pltpu.VMEM(flat, F32),
            pltpu.VMEM((2, 2, half + 1, rows), I32),
            pltpu.VMEM((2, 2 * OUTER, half + 1, rows), I32),
            pltpu.VMEM((2, 2, half + 1, rows), I32),
            pltpu.VMEM((2, MIDDLE, half + 1, rows), I32),
            pltpu.VMEM((2, 2, half, rows), F32),
            pltpu.VMEM((2, 2, 2, half, rows), F32),
            pltpu.VMEM((cases, part // 2 + 1, rows), I32),
            pltpu.VMEM((cases, part // 2 + 1, rows), I32),
            pltpu.VMEM((part // 2 + 1, rows), I32),
            pltpu.VMEM((cases, part // 2 + 1, rows), I32),
            pltpu.SemaphoreType.DMA((8,)),
            pltpu.SemaphoreType.DMA((2,)),
            pltpu.SemaphoreType.DMA((8,)),
            pltpu.SemaphoreType.DMA((8,)),
        ],
        compiler_params=pltpu.CompilerParams(
            collective_id=0, has_side_effects=True, vmem_limit_bytes=60 * 1024 * 1024
        ),
    )(
        forcing.reshape(flat),
        viscosity.reshape(flat),
        measured.reshape(flat),
        correction.reshape(flat),
        wall_rows,
        jnp.asarray(high),
        jnp.asarray(low),
        jnp.asarray(modes),
    )
    return pressure.reshape(forcing.shape), gradient.reshape(correction.shape)


def solution(mesh):
    return jax.shard_map(
        shards,
        mesh=mesh,
        in_specs=(
            P("case", "space", None, None),
            P("case", "space", None, None),
            P("case", "space", None, None),
            P("space", None, None),
            P("case", None),
        ),
        out_specs=(P("case", "space", None, None), P("space", None, None)),
        check_vma=False,
    )
```

```python
import functools

import jax
import jax.numpy as jnp
import ml_dtypes
import numpy as np
from jax import lax
from jax.experimental import pallas as pl
from jax.experimental.pallas import tpu as pltpu
from jax.sharding import PartitionSpec as P

MESH = pl.DeviceIdType.MESH
F32, BF16, I32 = jnp.float32, jnp.bfloat16, jnp.int32
OUTER, MIDDLE = 4, 4
TOP = 32767.0
LANES = 128
LIMIT = 16


def sine_tables(rows):
    index = np.arange(1, rows + 1, dtype=np.float64)
    phase = (index[:, None] * index[None, :]) % (2 * (rows + 1))
    sine = np.sqrt(2.0 / (rows + 1)) * np.sin(np.pi * phase / (rows + 1))
    high = sine.astype(ml_dtypes.bfloat16)
    low = (sine - high.astype(np.float64)).astype(ml_dtypes.bfloat16)
    return high, low


def mode_table(rows, cells, length, screen):
    index = np.arange(1, rows + 1, dtype=np.float64)
    centre = 4.0 * np.sin(np.pi * index / (2 * (rows + 1))) ** 2 + screen * screen
    rate = 1.0 + centre / 2.0 - np.sqrt(centre + centre * centre / 4.0)
    block = rate**cells
    lines = [
        rate,
        block,
        block**2,
        block ** (2 * MIDDLE),
        block ** (2 * MIDDLE * (OUTER - 1)),
        1.0 / (1.0 - rate**length),
        screen / (1.0 / rate - rate),
        np.zeros(rows),
    ]
    return np.stack(lines).astype(np.float32)


def wait_bytes(ref, sem):
    pltpu.make_async_copy(ref, ref, sem).wait()


def pack(first, second):
    largest = jnp.max(jnp.maximum(jnp.abs(first), jnp.abs(second)), axis=0, keepdims=True)
    code = jnp.ceil(jnp.log2(jnp.maximum(largest, 1e-30)) * 64.0)
    factor = TOP * jnp.exp2(code * (-1.0 / 64.0))
    a = jnp.round(first * factor).astype(I32)
    b = jnp.round(second * factor).astype(I32)
    return (a << 16) | (b & 0xFFFF), code.astype(I32)


def put(ref, first, second):
    words, code = pack(first, second)
    count, groups = words.shape[0], words.shape[1] // LANES
    for g in range(groups):
        ref[g * count : (g + 1) * count, :] = words[:, g * LANES : (g + 1) * LANES]
        ref[groups * count + g : groups * count + g + 1, :] = code[:, g * LANES : (g + 1) * LANES]


def take(ref, groups):
    count = ref.shape[0] // groups - 1
    first, second = [], []
    for g in range(groups):
        code = ref[groups * count + g : groups * count + g + 1, :]
        scale = jnp.exp2(code.astype(F32) * (1.0 / 64.0)) * (1.0 / TOP)
        words = ref[g * count : (g + 1) * count, :]
        first.append((words >> 16).astype(F32) * scale)
        second.append(((words << 16) >> 16).astype(F32) * scale)
    return jnp.concatenate(first, axis=1), jnp.concatenate(second, axis=1)


def kernel(cases, cells, planes, rows, forcing_in, viscosity_in, measured_in, correction_in, walls_in, high_in, low_in,
           modes_in, pressure_out, words_out, forcing, viscosity, measured, correction, walls, high_ref, low_ref, modes,
           head, tail, spectrum, result, moments, pressure, xs_send, xs_got, hs_send, hs_got, cs_send, cs_got,
           rs_send, rs_got, ag_send, in_sems, out_sems, sends, recvs):
    me = lax.axis_index("space")
    case = lax.axis_index("case")
    inner, middle, outer = me % 2, me // 2 % MIDDLE, me // (2 * MIDDLE)
    half = planes // 2
    groups = rows // LANES
    is_first = inner == 0

    def space(o, m, i):
        return {"space": (o * MIDDLE + m) * 2 + i}

    barrier = pltpu.get_barrier_semaphore()

    def greet(device):
        pl.semaphore_signal(barrier, inc=1, device_id=device, device_id_type=MESH)

    for k in (2, 1, 3):
        greet(space(outer, (middle + k) % MIDDLE, inner))
    loads = [
        pltpu.make_async_copy(src, dst, in_sems.at[i])
        for i, (src, dst) in enumerate(
            (
                (forcing_in, forcing),
                (viscosity_in, viscosity),
                (correction_in, correction),
                (high_in, high_ref),
                (low_in, low_ref),
                (modes_in, modes),
                (walls_in, walls),
                (measured_in, measured),
            )
        )
    ]
    for load in loads:
        load.start()
    for k in range(1, cases):
        greet({"case": (case + k) % cases})
    for k in range(1, 2 * OUTER):
        greet(space((outer + k // 2) % OUTER, middle, (inner + k) % 2))

    def lines(h, i):
        return pl.ds(pl.multiple_of(i * planes + h * half, half), half)

    def split(h, i, value):
        top = value.astype(BF16)
        head[h, i * half : (i + 1) * half, :] = top
        tail[h, i * half : (i + 1) * half, :] = (value - top.astype(F32)).astype(BF16)

    def sine(h):
        high, low = high_ref[...], low_ref[...]
        top = head[h]
        small = jnp.dot(top, low, preferred_element_type=F32) + jnp.dot(tail[h], high, preferred_element_type=F32)
        return jnp.dot(top, high, preferred_element_type=F32) + small

    def at(ref, h, i):
        return ref[h, i * half : (i + 1) * half, :]

    def line(i):
        return modes[i : i + 1, :]

    def send(src, dst, phase, device):
        pltpu.make_async_remote_copy(
            src_ref=src, dst_ref=dst, send_sem=sends.at[phase], recv_sem=recvs.at[phase], device_id=device, device_id_type=MESH
        ).start()

    def begin(turn, h):
        spectrum[h] = sine(h)
        rate = line(0)
        onward = rate * at(spectrum, h, 0)
        backward = rate * at(spectrum, h, cells - 1)
        for i in range(1, cells):
            onward = (onward + at(spectrum, h, i)) * rate
            backward = (backward + at(spectrum, h, cells - 1 - i)) * rate
        moments[0, h] = onward
        moments[1, h] = backward
        put(xs_send.at[turn, h], onward, backward)

    def send_moments(turn, h, steps):
        for d in steps:
            send(
                xs_send.at[turn, h], xs_got.at[turn, 2 * outer + inner], 3 * turn, space((outer + d) % OUTER, middle, h)
            )

    def cross(turn):
        first = 3 * turn
        wait_bytes(xs_got.at[turn, pl.ds(0, 2 * OUTER - 1)], recvs.at[first])
        block, two, eight, most = line(1), line(2), line(3), line(4)
        own_l, own_r = moments[0, inner], moments[1, inner]
        other_l, other_r = take(xs_got.at[turn, 2 * outer + 1 - inner], groups)
        l0, l1 = jnp.where(is_first, own_l, other_l), jnp.where(is_first, other_l, own_l)
        r0, r1 = jnp.where(is_first, own_r, other_r), jnp.where(is_first, other_r, own_r)
        chip_l, chip_r = l0 * block + l1, r0 + r1 * block
        pairs = []
        for d in range(1, OUTER):
            slot = 2 * ((outer + d) % OUTER)
            a_l, a_r = take(xs_got.at[turn, slot], groups)
            b_l, b_r = take(xs_got.at[turn, slot + 1], groups)
            pairs.append((a_l * block + b_l, a_r + b_r * block))
        before = pairs[0][0]
        after = pairs[OUTER - 2][1]
        for d in range(1, OUTER - 1):
            before = pairs[d][0] + eight * before
            after = pairs[OUTER - 2 - d][1] + eight * after
        onto, round_l = chip_l + eight * before, before + most * chip_l
        back, round_r = chip_r + eight * after, after + most * chip_r
        put(hs_send.at[turn, 0], onto, round_r)
        put(hs_send.at[turn, 1], round_l, back)
        for k in (2, 1, 3):
            send(
                hs_send.at[turn, (middle + k) // MIDDLE],
                hs_got.at[turn, middle],
                first + 1,
                space(outer, (middle + k) % MIDDLE, inner),
            )
        wait_bytes(hs_got.at[turn, pl.ds(0, MIDDLE - 1)], recvs.at[first + 1])
        near = [take(hs_got.at[turn, (middle + d) % MIDDLE], groups) for d in range(1, MIDDLE)]
        left, right = round_l, round_r
        for d in range(1, MIDDLE):
            left = near[d - 1][0] + two * left
            right = near[MIDDLE - 1 - d][1] + two * right
        left, right = left * line(5), right * line(5)
        left_1, right_0 = left * block + l0, right * block + r1
        cs_send[turn, 0] = jnp.where(is_first, left_1, left)
        cs_send[turn, 1] = jnp.where(is_first, right, right_0)
        send(cs_send.at[turn], cs_got.at[turn], first + 2, space(outer, middle, 1 - inner))
        return jnp.where(is_first, left, left_1), jnp.where(is_first, right_0, right)

    def finish(h, left, right):
        rate = line(0)
        running = right
        for i in range(cells - 1, -1, -1):
            result[h, i * half : (i + 1) * half, :] = running
            running = (running + at(spectrum, h, i)) * rate
        running = left
        for i in range(cells):
            running = at(spectrum, h, i) + (running if i == 0 else running * rate)
            split(h, i, (running + at(result, h, i)) * line(6))
        result[h] = sine(h)

    def misfit(h):
        chosen = lax.broadcasted_iota(I32, (half, planes), 0) + h * half == lax.broadcasted_iota(I32, (half, planes), 1)
        first_row = jnp.sum(jnp.where(chosen, walls[...], 0), axis=1, keepdims=True)
        outside = lax.broadcasted_iota(I32, (half, rows), 1) >= first_row
        for i in range(cells):
            value = at(result, h, i)
            pressure[lines(h, i), :] = value
            split(h, i, jnp.where(outside, value - measured[lines(h, i), :].astype(F32), 0.0))

    def give(h):
        for i in range(cells):
            value = viscosity[lines(h, i), :].astype(F32) * at(result, h, i)
            put(rs_send.at[h * cells + i], value[: half // 2], value[half // 2 :])
        for k in range(cells):
            other = h * cells + (case + k) % cells

            @pl.when(other != case)
            def _():
                send(rs_send.at[other], rs_got.at[case], 6, {"case": other})

    for i in range(3):
        loads[i].wait()
    for i in range(cells):
        for h in range(2):
            rows_in = lines(h, i)
            split(h, i, forcing[rows_in, :].astype(F32) + viscosity[rows_in, :].astype(F32) * correction[rows_in, :])
    for i in range(3, 8):
        loads[i].wait()
    for h in range(2):
        begin(0, h)
    pl.semaphore_wait(barrier, cases - 1 + MIDDLE - 1 + 2 * OUTER - 1)
    send_moments(0, inner, (2, 1, 3))
    send_moments(0, 1 - inner, (2, 1, 3, 0))
    left, right = cross(0)
    finish(inner, left, right)
    misfit(inner)
    begin(1, inner)
    send_moments(1, inner, (2, 1, 3))
    wait_bytes(cs_got.at[0], recvs.at[2])
    finish(1 - inner, cs_got[0, 0], cs_got[0, 1])
    misfit(1 - inner)
    begin(1, 1 - inner)
    send_moments(1, 1 - inner, (2, 1, 3, 0))
    copy_out = pltpu.make_async_copy(pressure, pressure_out, out_sems.at[0])
    copy_out.start()
    left, right = cross(1)
    finish(inner, left, right)
    give(inner)
    wait_bytes(cs_got.at[1], recvs.at[5])
    finish(1 - inner, cs_got[1, 0], cs_got[1, 1])
    give(1 - inner)
    rs_got[case] = rs_send[case]
    for turn in range(2):
        wait_bytes(xs_got.at[turn, pl.ds(0, 2 * OUTER - 1)], sends.at[3 * turn])
        wait_bytes(hs_got.at[turn, pl.ds(0, MIDDLE - 1)], sends.at[3 * turn + 1])
        wait_bytes(cs_got.at[turn], sends.at[3 * turn + 2])
    copy_out.wait()
    wait_bytes(rs_got.at[pl.ds(0, cases - 1)], recvs.at[6])
    upper, lower = take(rs_got.at[0], groups)
    for k in range(1, cases):
        a, b = take(rs_got.at[k], groups)
        upper, lower = upper + a, lower + b
    put(ag_send, upper, lower)
    for k in range(1, cases):
        send(ag_send, words_out.at[case], 7, {"case": (case + k) % cases})
    keep = pltpu.make_async_copy(ag_send, words_out.at[case], out_sems.at[1])
    keep.start()
    wait_bytes(rs_got.at[pl.ds(0, cases - 1)], sends.at[6])
    keep.wait()
    wait_bytes(words_out.at[pl.ds(0, cases - 1)], recvs.at[7])
    wait_bytes(words_out.at[pl.ds(0, cases - 1)], sends.at[7])


def spread(cells, planes, pressure_in, words, pressure_out, gradient_out, gradient, sems):
    copies = [pltpu.make_async_copy(pressure_in, pressure_out, sems.at[0])]
    copies[0].start()
    half = planes // 2
    for h in range(2):
        for i in range(cells):
            a, b = take(words.at[h * cells + i], gradient.shape[1] // LANES)
            start = i * planes + h * half
            gradient[start : start + half // 2, :] = a
            gradient[start + half // 2 : start + half, :] = b
    copies.append(pltpu.make_async_copy(gradient, gradient_out, sems.at[1]))
    copies[1].start()
    for copy in copies:
        copy.wait()


def shards(forcing, viscosity, measured, correction, wall_rows):
    cells, planes, rows = correction.shape
    spaces, cases = lax.axis_size("space"), lax.axis_size("case")
    assert spaces == 2 * OUTER * MIDDLE and cases == 2 * cells
    high, low = sine_tables(rows)
    modes = mode_table(rows, cells, cells * spaces, 1.0 / (2.0 * cells))
    flat = (cells * planes, rows)
    half, groups = planes // 2, rows // LANES
    halves = (2, cells * half, rows)
    message = (groups * (half + 1), LANES)
    short = (groups * (half // 2 + 1), LANES)
    there = pl.BlockSpec(memory_space=pltpu.HBM)
    anywhere = pl.BlockSpec(memory_space=pl.ANY)
    pressure, words = pl.pallas_call(
        functools.partial(kernel, cases, cells, planes, rows),
        out_shape=(jax.ShapeDtypeStruct(flat, F32), jax.ShapeDtypeStruct((cases, *short), I32)),
        in_specs=[there] * 8,
        out_specs=(anywhere,) * 2,
        scratch_shapes=[
            pltpu.VMEM(flat, BF16),
            pltpu.VMEM(flat, BF16),
            pltpu.VMEM(flat, BF16),
            pltpu.VMEM(flat, F32),
            pltpu.VMEM((1, planes), I32),
            pltpu.VMEM((rows, rows), BF16),
            pltpu.VMEM((rows, rows), BF16),
            pltpu.VMEM(modes.shape, F32),
            pltpu.VMEM(halves, BF16),
            pltpu.VMEM(halves, BF16),
            pltpu.VMEM(halves, F32),
            pltpu.VMEM(halves, F32),
            pltpu.VMEM((2, 2, half, rows), F32),
            pltpu.VMEM(flat, F32),
            pltpu.VMEM((2, 2, *message), I32),
            pltpu.VMEM((2, 2 * OUTER, *message), I32),
            pltpu.VMEM((2, 2, *message), I32),
            pltpu.VMEM((2, MIDDLE, *message), I32),
            pltpu.VMEM((2, 2, half, rows), F32),
            pltpu.VMEM((2, 2, half, rows), F32),
            pltpu.VMEM((cases, *short), I32),
            pltpu.VMEM((cases, *short), I32),
            pltpu.VMEM(short, I32),
            pltpu.SemaphoreType.DMA((8,)),
            pltpu.SemaphoreType.DMA((2,)),
            pltpu.SemaphoreType.DMA((8,)),
            pltpu.SemaphoreType.DMA((8,)),
        ],
        compiler_params=pltpu.CompilerParams(
            collective_id=0, has_side_effects=True, vmem_limit_bytes=LIMIT * 1024 * 1024
        ),
    )(
        *(pltpu.with_memory_space_constraint(x, pltpu.HBM) for x in (forcing.reshape(flat),
        viscosity.reshape(flat),
        measured.reshape(flat),
        correction.reshape(flat),
        wall_rows,
        jnp.asarray(high),
        jnp.asarray(low),
        jnp.asarray(modes))),
    )
    pressure, gradient = pl.pallas_call(
        functools.partial(spread, cells, planes),
        out_shape=(jax.ShapeDtypeStruct(flat, F32), jax.ShapeDtypeStruct(flat, F32)),
        in_specs=[anywhere, pl.BlockSpec(memory_space=pltpu.VMEM)],
        out_specs=(anywhere,) * 2,
        scratch_shapes=[pltpu.VMEM(flat, F32), pltpu.SemaphoreType.DMA((2,))],
        compiler_params=pltpu.CompilerParams(vmem_limit_bytes=LIMIT * 1024 * 1024),
    )(pressure, words)
    return pressure.reshape(forcing.shape), gradient.reshape(correction.shape)


def solution(mesh):
    return jax.shard_map(
        shards,
        mesh=mesh,
        in_specs=(
            P("case", "space", None, None),
            P("case", "space", None, None),
            P("case", "space", None, None),
            P("space", None, None),
            P("case", None),
        ),
        out_specs=(P("case", "space", None, None), P("space", None, None)),
        check_vma=False,
    )
```

```python
import functools

import jax
import jax.numpy as jnp
import ml_dtypes
import numpy as np
from jax import lax
from jax.experimental import pallas as pl
from jax.experimental.pallas import tpu as pltpu
from jax.sharding import PartitionSpec as P

MESH = pl.DeviceIdType.MESH
F32, BF16, I32 = jnp.float32, jnp.bfloat16, jnp.int32
OUTER, MIDDLE = 4, 4
TOP = 32767.0
LANES = 128
LIMIT = 16


def sine_tables(rows):
    index = np.arange(1, rows + 1, dtype=np.float64)
    phase = (index[:, None] * index[None, :]) % (2 * (rows + 1))
    sine = np.sqrt(2.0 / (rows + 1)) * np.sin(np.pi * phase / (rows + 1))
    high = sine.astype(ml_dtypes.bfloat16)
    low = (sine - high.astype(np.float64)).astype(ml_dtypes.bfloat16)
    return high, low


def mode_table(rows, cells, length, screen):
    index = np.arange(1, rows + 1, dtype=np.float64)
    centre = 4.0 * np.sin(np.pi * index / (2 * (rows + 1))) ** 2 + screen * screen
    rate = 1.0 + centre / 2.0 - np.sqrt(centre + centre * centre / 4.0)
    lines = [rate, 1.0 / (1.0 - rate**length), screen / (1.0 / rate - rate)]
    step = 1
    while step < length // cells:
        lines.append(rate ** (cells * step))
        step *= 2
    table = np.zeros((-(-len(lines) // 8) * 8, rows))
    table[: len(lines)] = lines
    return table.astype(np.float32)


def wait_bytes(ref, sem):
    pltpu.make_async_copy(ref, ref, sem).wait()


def pack(first, second):
    largest = jnp.max(jnp.maximum(jnp.abs(first), jnp.abs(second)), axis=0, keepdims=True)
    code = jnp.ceil(jnp.log2(jnp.maximum(largest, 1e-30)) * 64.0)
    factor = TOP * jnp.exp2(code * (-1.0 / 64.0))
    a = jnp.round(first * factor).astype(I32)
    b = jnp.round(second * factor).astype(I32)
    return (a << 16) | (b & 0xFFFF), code.astype(I32)


def put(ref, first, second):
    words, code = pack(first, second)
    count, groups = words.shape[0], words.shape[1] // LANES
    for g in range(groups):
        ref[g * count : (g + 1) * count, :] = words[:, g * LANES : (g + 1) * LANES]
        ref[groups * count + g : groups * count + g + 1, :] = code[:, g * LANES : (g + 1) * LANES]


def take(ref, groups):
    count = ref.shape[0] // groups - 1
    first, second = [], []
    for g in range(groups):
        code = ref[groups * count + g : groups * count + g + 1, :]
        scale = jnp.exp2(code.astype(F32) * (1.0 / 64.0)) * (1.0 / TOP)
        words = ref[g * count : (g + 1) * count, :]
        first.append((words >> 16).astype(F32) * scale)
        second.append(((words << 16) >> 16).astype(F32) * scale)
    return jnp.concatenate(first, axis=1), jnp.concatenate(second, axis=1)


def kernel(cases, cells, planes, rows, forcing_in, viscosity_in, measured_in, correction_in, walls_in, high_in, low_in,
           modes_in, pressure_out, words_out, forcing, viscosity, measured, correction, walls, high_ref, low_ref, modes,
           head, tail, spectrum, result, pressure, walls_send, walls_got, a_send, a_got, b_send, b_got,
           rs_send, rs_got, ag_send, in_sems, out_sems, sends, recvs):
    me = lax.axis_index("space")
    case = lax.axis_index("case")
    inner, middle, outer = me % 2, me // 2 % MIDDLE, me // (2 * MIDDLE)
    half = planes // 2
    groups = rows // LANES
    spaces = 2 * OUTER * MIDDLE
    partner = (case + cases // 2) % cases
    upper_case = case // (cases // 2)
    owned = (outer * MIDDLE + (middle + MIDDLE - 1 + upper_case) % MIDDLE) * 2 + inner

    def solver(plane):
        o, m, i = plane // (2 * MIDDLE), plane // 2 % MIDDLE, plane % 2
        return {"case": partner, "space": (o * MIDDLE + (m + upper_case) % MIDDLE) * 2 + i}

    def nearby(steps):
        return [(o, m, i) for m in steps for o in (2, 1, 3, 0) for i in (1, 0)]

    barrier = pltpu.get_barrier_semaphore()

    def greet(device):
        pl.semaphore_signal(barrier, inc=1, device_id=device, device_id_type=MESH)

    def place(o, m, i):
        return (((outer + o) % OUTER) * MIDDLE + (middle + m) % MIDDLE) * 2 + (inner + i) % 2

    loads = [
        pltpu.make_async_copy(src, dst, in_sems.at[i])
        for i, (src, dst) in enumerate(
            (
                (forcing_in, forcing),
                (viscosity_in, viscosity),
                (correction_in, correction),
                (high_in, high_ref),
                (low_in, low_ref),
                (modes_in, modes),
                (walls_in, walls),
                (measured_in, measured),
            )
        )
    ]
    for load in loads[:3]:
        load.start()
    for o, m, i in nearby((1, 2, 3, 0)):
        greet({"case": partner, "space": place(o, m + upper_case, i)})
    for load in loads[3:]:
        load.start()
    for k in range(1, cases):
        greet({"case": (case + k) % cases})

    def lines(h, i):
        start = i * planes + h * half
        return slice(start, start + half)

    def split(h, i, value):
        count = value.shape[0]
        top = value.astype(BF16)
        head[h, i * count : (i + 1) * count, :] = top
        tail[h, i * count : (i + 1) * count, :] = (value - top.astype(F32)).astype(BF16)

    def sine(h):
        high, low = high_ref[...], low_ref[...]
        top = head[h]
        small = jnp.dot(top, low, preferred_element_type=F32) + jnp.dot(tail[h], high, preferred_element_type=F32)
        return jnp.dot(top, high, preferred_element_type=F32) + small

    def at(ref, h, i):
        return ref[h, i * half : (i + 1) * half, :]

    def line(i):
        return modes[i : i + 1, :]

    def send(src, dst, phase, device):
        pltpu.make_async_remote_copy(
            src_ref=src, dst_ref=dst, send_sem=sends.at[phase], recv_sem=recvs.at[phase], device_id=device, device_id_type=MESH
        ).start()

    def lay(ref, where, k, value):
        for g in range(groups):
            ref[where, k * groups + g, :] = value[:, g * LANES : (g + 1) * LANES]

    def lift(ref, where, k):
        return jnp.concatenate([ref[where, k * groups + g, :] for g in range(groups)], axis=1)

    def block_moments(ref, h):
        rate = line(0)
        onward = rate * at(ref, h, 0)
        backward = rate * at(ref, h, cells - 1)
        for i in range(1, cells):
            onward = (onward + at(ref, h, i)) * rate
            backward = (backward + at(ref, h, cells - 1 - i)) * rate
        return onward, backward

    def finish(ref, h, left=None, right=None):
        rate = line(0)
        running = right
        for i in range(cells - 1, -1, -1):
            if running is not None:
                result[h, i * half : (i + 1) * half, :] = running
            running = (at(ref, h, i) if running is None else running + at(ref, h, i)) * rate
        running = left
        for i in range(cells):
            value = at(ref, h, i)
            running = value if running is None else value + (running if i == 0 else running * rate)
            full = running if right is None and i == cells - 1 else running + at(result, h, i)
            split(h, i, full * line(2))
        result[h] = sine(h)

    def misfit(h, keep):
        chosen = lax.broadcasted_iota(I32, (half, planes), 0) + h * half == lax.broadcasted_iota(I32, (half, planes), 1)
        first_row = jnp.sum(jnp.where(chosen, walls[...], 0), axis=1, keepdims=True)
        outside = lax.broadcasted_iota(I32, (half, rows), 1) >= first_row
        for i in range(cells):
            value = at(result, h, i)
            if keep:
                pressure[lines(h, i), :] = value
            split(h, i, jnp.where(outside, value - measured[lines(h, i), :].astype(F32), 0.0))

    def give(h):
        for i in range(cells):
            value = viscosity[lines(h, i), :].astype(F32) * at(result, h, i)
            put(rs_send.at[h * cells + i], value[: half // 2], value[half // 2 :])
        for k in range(cells):
            other = h * cells + (case + k) % cells

            @pl.when(other != case)
            def _():
                send(rs_send.at[other], rs_got.at[case], 2, {"case": other})

    for i in range(3):
        loads[i].wait()
    for h in range(2):
        for i in range(cells):
            part = lines(h, i)
            split(h, i, forcing[part, :].astype(F32) + viscosity[part, :].astype(F32) * correction[part, :])
    for i in range(3, 8):
        loads[i].wait()
    walls_send[...] = jnp.zeros_like(walls_send)
    walls_send[:, 0:planes] = walls[...]
    for h in range(2):
        some = slice(h * half, (h + 1) * half)
        spectrum[h] = sine(h)
        onward, backward = block_moments(spectrum, h)
        lay(a_send, some, 0, onward)
        lay(a_send, some, 1, backward)
        finish(spectrum, h)
        misfit(h, False)
        result[h] = sine(h)
        onward, backward = block_moments(result, h)
        lay(a_send, some, 2, onward)
        lay(a_send, some, 3, backward)
    pl.semaphore_wait(barrier, cases - 1 + spaces)
    send(walls_send, walls_got, 4, solver(me))
    for o, m, i in nearby((1, 2, 3, 0)):
        plane = place(o, m, i)
        send(a_send.at[plane], a_got.at[me], 0, solver(plane))

    wait_bytes(walls_got, recvs.at[4])
    chosen = lax.broadcasted_iota(I32, walls_got.shape, 1) == owned
    first_row = jnp.sum(jnp.where(chosen, walls_got[...], 0), axis=1, keepdims=True)
    outside = lax.broadcasted_iota(I32, (1, rows), 1) >= first_row
    wait_bytes(a_got, recvs.at[0])
    every = slice(0, spaces)

    def scan(onward, backward):
        step, k = 1, 3
        while step < spaces:
            onward = onward + line(k) * pltpu.roll(onward, step, 0)
            backward = backward + line(k) * pltpu.roll(backward, spaces - step, 0)
            step, k = 2 * step, k + 1
        return pltpu.roll(onward, 1, 0) * line(1), pltpu.roll(backward, spaces - 1, 0) * line(1)

    rate = line(0)
    left, right = scan(lift(a_got, every, 0), lift(a_got, every, 1))
    lay(b_send, every, 0, left)
    lay(b_send, every, 1, right)
    quarter = cells // 2
    powers = [line(2)]
    for i in range(1, cells):
        powers.append(powers[-1] * rate)
    for i in range(cells):
        split(i // quarter, i % quarter, left * powers[i] + right * powers[cells - 1 - i])

    def row_block(i):
        return result[i // quarter, (i % quarter) * spaces : (i % quarter + 1) * spaces, :]

    for h in range(2):
        result[h] = sine(h)
    for i in range(cells):
        split(i // quarter, i % quarter, jnp.where(outside, row_block(i), 0.0))
    for h in range(2):
        result[h] = sine(h)
    onward, backward = rate * row_block(0), rate * row_block(cells - 1)
    for i in range(1, cells):
        onward = (onward + row_block(i)) * rate
        backward = (backward + row_block(cells - 1 - i)) * rate
    left, right = scan(lift(a_got, every, 2) + onward, lift(a_got, every, 3) + backward)
    lay(b_send, every, 2, left)
    lay(b_send, every, 3, right)
    for o, m, i in nearby((1, 2, 3, 0)):
        target = place(o, m + upper_case, i)
        send(b_send.at[target], b_got.at[owned], 1, {"case": partner, "space": target})
    wait_bytes(b_got, recvs.at[1])

    for h in range(2):
        some = slice(h * half, (h + 1) * half)
        finish(spectrum, h, lift(b_got, some, 0), lift(b_got, some, 1))
        misfit(h, True)
        spectrum[h] = sine(h)
        finish(spectrum, h, lift(b_got, some, 2), lift(b_got, some, 3))
        give(h)
    copy_out = pltpu.make_async_copy(pressure, pressure_out, out_sems.at[0])
    copy_out.start()
    rs_got[case] = rs_send[case]
    wait_bytes(a_got, sends.at[0])
    wait_bytes(b_got, sends.at[1])
    wait_bytes(walls_got, sends.at[4])
    wait_bytes(rs_got.at[pl.ds(0, cases - 1)], recvs.at[2])
    upper, lower = take(rs_got.at[0], groups)
    for k in range(1, cases):
        a, b = take(rs_got.at[k], groups)
        upper, lower = upper + a, lower + b
    put(ag_send, upper, lower)
    for k in range(1, cases):
        send(ag_send, words_out.at[case], 3, {"case": (case + k) % cases})
    keep = pltpu.make_async_copy(ag_send, words_out.at[case], out_sems.at[1])
    keep.start()
    wait_bytes(rs_got.at[pl.ds(0, cases - 1)], sends.at[2])
    copy_out.wait()
    keep.wait()
    wait_bytes(words_out.at[pl.ds(0, cases - 1)], recvs.at[3])
    wait_bytes(words_out.at[pl.ds(0, cases - 1)], sends.at[3])


def spread(cells, planes, pressure_in, words, pressure_out, gradient_out, gradient, sems):
    copies = [pltpu.make_async_copy(pressure_in, pressure_out, sems.at[0])]
    copies[0].start()
    half = planes // 2
    for h in range(2):
        for i in range(cells):
            a, b = take(words.at[h * cells + i], gradient.shape[1] // LANES)
            start = i * planes + h * half
            gradient[start : start + half // 2, :] = a
            gradient[start + half // 2 : start + half, :] = b
    copies.append(pltpu.make_async_copy(gradient, gradient_out, sems.at[1]))
    copies[1].start()
    for copy in copies:
        copy.wait()


def shards(forcing, viscosity, measured, correction, wall_rows):
    cells, planes, rows = correction.shape
    spaces, cases = lax.axis_size("space"), lax.axis_size("case")
    assert spaces == 2 * OUTER * MIDDLE and cases == 2 * cells
    high, low = sine_tables(rows)
    modes = mode_table(rows, cells, cells * spaces, 1.0 / (2.0 * cells))
    flat = (cells * planes, rows)
    half, groups = planes // 2, rows // LANES
    halves = (2, cells * half, rows)
    short = (groups * (half // 2 + 1), LANES)
    there = pl.BlockSpec(memory_space=pltpu.HBM)
    anywhere = pl.BlockSpec(memory_space=pl.ANY)
    pressure, words = pl.pallas_call(
        functools.partial(kernel, cases, cells, planes, rows),
        out_shape=(jax.ShapeDtypeStruct(flat, F32), jax.ShapeDtypeStruct((cases, *short), I32)),
        in_specs=[there] * 8,
        out_specs=(anywhere,) * 2,
        scratch_shapes=[
            pltpu.VMEM(flat, BF16),
            pltpu.VMEM(flat, BF16),
            pltpu.VMEM(flat, BF16),
            pltpu.VMEM(flat, F32),
            pltpu.VMEM((1, planes), I32),
            pltpu.VMEM((rows, rows), BF16),
            pltpu.VMEM((rows, rows), BF16),
            pltpu.VMEM(modes.shape, F32),
            pltpu.VMEM(halves, BF16),
            pltpu.VMEM(halves, BF16),
            pltpu.VMEM(halves, F32),
            pltpu.VMEM(halves, F32),
            pltpu.VMEM(flat, F32),
            pltpu.VMEM((1, LANES), I32),
            pltpu.VMEM((1, LANES), I32),
            *[pltpu.VMEM((spaces, 4 * groups, LANES), F32)] * 4,
            pltpu.VMEM((cases, *short), I32),
            pltpu.VMEM((cases, *short), I32),
            pltpu.VMEM(short, I32),
            pltpu.SemaphoreType.DMA((8,)),
            pltpu.SemaphoreType.DMA((2,)),
            pltpu.SemaphoreType.DMA((5,)),
            pltpu.SemaphoreType.DMA((5,)),
        ],
        compiler_params=pltpu.CompilerParams(
            collective_id=0, has_side_effects=True, vmem_limit_bytes=LIMIT * 1024 * 1024
        ),
    )(
        *(pltpu.with_memory_space_constraint(x, pltpu.HBM) for x in (forcing.reshape(flat),
        viscosity.reshape(flat),
        measured.reshape(flat),
        correction.reshape(flat),
        wall_rows,
        jnp.asarray(high),
        jnp.asarray(low),
        jnp.asarray(modes))),
    )
    pressure, gradient = pl.pallas_call(
        functools.partial(spread, cells, planes),
        out_shape=(jax.ShapeDtypeStruct(flat, F32), jax.ShapeDtypeStruct(flat, F32)),
        in_specs=[anywhere, pl.BlockSpec(memory_space=pltpu.VMEM)],
        out_specs=(anywhere,) * 2,
        scratch_shapes=[pltpu.VMEM(flat, F32), pltpu.SemaphoreType.DMA((2,))],
        compiler_params=pltpu.CompilerParams(vmem_limit_bytes=LIMIT * 1024 * 1024),
    )(pressure, words)
    return pressure.reshape(forcing.shape), gradient.reshape(correction.shape)


def solution(mesh):
    return jax.shard_map(
        shards,
        mesh=mesh,
        in_specs=(
            P("case", "space", None, None),
            P("case", "space", None, None),
            P("case", "space", None, None),
            P("space", None, None),
            P("case", None),
        ),
        out_specs=(P("case", "space", None, None), P("space", None, None)),
        check_vma=False,
    )
```

```python
import functools

import jax
import jax.numpy as jnp
import ml_dtypes
import numpy as np
from jax import lax
from jax.experimental import pallas as pl
from jax.experimental.pallas import tpu as pltpu
from jax.sharding import PartitionSpec as P

MESH = pl.DeviceIdType.MESH
F32, BF16, I32 = jnp.float32, jnp.bfloat16, jnp.int32
OUTER, MIDDLE = 4, 4
TOP = 32767.0
LANES = 128
SEGMENT = 16
LIMIT = 16


def sine_tables(rows):
    index = np.arange(1, rows + 1, dtype=np.float64)
    phase = (index[:, None] * index[None, :]) % (2 * (rows + 1))
    sine = np.sqrt(2.0 / (rows + 1)) * np.sin(np.pi * phase / (rows + 1))
    high = sine.astype(ml_dtypes.bfloat16)
    low = (sine - high.astype(np.float64)).astype(ml_dtypes.bfloat16)
    return high, low


def mode_table(rows, cells, length, screen):
    index = np.arange(1, rows + 1, dtype=np.float64)
    centre = 4.0 * np.sin(np.pi * index / (2 * (rows + 1))) ** 2 + screen * screen
    rate = 1.0 + centre / 2.0 - np.sqrt(centre + centre * centre / 4.0)
    lines = [rate, 1.0 / (1.0 - rate**length), screen / (1.0 / rate - rate)]
    step = 1
    while step < length // cells:
        lines.append(rate ** (cells * step))
        step *= 2
    table = np.zeros((-(-len(lines) // 8) * 8, rows))
    table[: len(lines)] = lines
    return table.astype(np.float32)


def wait_bytes(ref, sem):
    pltpu.make_async_copy(ref, ref, sem).wait()


def pack(first, second):
    largest = jnp.max(jnp.maximum(jnp.abs(first), jnp.abs(second)), axis=0, keepdims=True)
    code = jnp.ceil(jnp.log2(jnp.maximum(largest, 1e-30)) * 64.0)
    factor = TOP * jnp.exp2(code * (-1.0 / 64.0))
    a = jnp.round(first * factor).astype(I32)
    b = jnp.round(second * factor).astype(I32)
    return (a << 16) | (b & 0xFFFF), code.astype(I32)


def put(ref, first, second):
    words, code = pack(first, second)
    count, groups = words.shape[0], words.shape[1] // LANES
    for g in range(groups):
        ref[g * count : (g + 1) * count, :] = words[:, g * LANES : (g + 1) * LANES]
        ref[groups * count + g : groups * count + g + 1, :] = code[:, g * LANES : (g + 1) * LANES]


def take(ref, groups):
    count = ref.shape[0] // groups - 1
    first, second = [], []
    for g in range(groups):
        code = ref[groups * count + g : groups * count + g + 1, :]
        scale = jnp.exp2(code.astype(F32) * (1.0 / 64.0)) * (1.0 / TOP)
        words = ref[g * count : (g + 1) * count, :]
        first.append((words >> 16).astype(F32) * scale)
        second.append(((words << 16) >> 16).astype(F32) * scale)
    return jnp.concatenate(first, axis=1), jnp.concatenate(second, axis=1)


def kernel(cases, cells, planes, rows, forcing_in, viscosity_in, measured_in, correction_in, walls_in, high_in, low_in,
           modes_in, pressure_out, words_out, forcing, viscosity, measured, correction, walls, high_ref, low_ref, modes,
           head, tail, spectrum, result, pressure, walls_send, walls_got, a_send, a_got, b_send, b_got,
           rs_send, rs_got, ag_send, in_sems, out_sems, sends, recvs):
    me = lax.axis_index("space")
    case = lax.axis_index("case")
    inner, middle, outer = me % 2, me // 2 % MIDDLE, me // (2 * MIDDLE)
    half = planes // 2
    groups = rows // LANES
    spaces = 2 * OUTER * MIDDLE
    partner = (case + cases // 2) % cases
    upper_case = case // (cases // 2)
    owned = (outer * MIDDLE + (middle + MIDDLE - 1 + upper_case) % MIDDLE) * 2 + inner

    def solver(plane):
        o, m, i = plane // (2 * MIDDLE), plane // 2 % MIDDLE, plane % 2
        return {"case": partner, "space": (o * MIDDLE + (m + upper_case) % MIDDLE) * 2 + i}

    def nearby(steps):
        return [(o, m, i) for m in steps for o in (2, 1, 3, 0) for i in (1, 0)]

    barrier = pltpu.get_barrier_semaphore()

    def greet(device):
        pl.semaphore_signal(barrier, inc=1, device_id=device, device_id_type=MESH)

    def place(o, m, i):
        return (((outer + o) % OUTER) * MIDDLE + (middle + m) % MIDDLE) * 2 + (inner + i) % 2

    loads = [
        pltpu.make_async_copy(src, dst, in_sems.at[i])
        for i, (src, dst) in enumerate(
            (
                (forcing_in, forcing),
                (viscosity_in, viscosity),
                (correction_in, correction),
                (high_in, high_ref),
                (low_in, low_ref),
                (modes_in, modes),
                (walls_in, walls),
                (measured_in, measured),
            )
        )
    ]
    for load in loads[:3]:
        load.start()
    for o, m, i in nearby((1, 2, 3, 0)):
        greet({"case": partner, "space": place(o, m + upper_case, i)})
    for load in loads[3:]:
        load.start()
    for k in range(1, cases):
        greet({"case": (case + k) % cases})

    def lines(h, i):
        return pl.ds(pl.multiple_of(i * planes + h * half, half), half)

    def case_at(far, step, y):
        bit = (case // 4 + step) % 2
        return (upper_case + far) % 2 * (cases // 2) + bit * 4 + (case + y) % 4

    def split(h, i, value):
        count = value.shape[0]
        top = value.astype(BF16)
        head[h, i * count : (i + 1) * count, :] = top
        tail[h, i * count : (i + 1) * count, :] = (value - top.astype(F32)).astype(BF16)

    def sine(h):
        high, low = high_ref[...], low_ref[...]
        top = head[h]
        small = jnp.dot(top, low, preferred_element_type=F32) + jnp.dot(tail[h], high, preferred_element_type=F32)
        return jnp.dot(top, high, preferred_element_type=F32) + small

    def at(ref, h, i):
        return ref[h, i * half : (i + 1) * half, :]

    def line(i):
        return modes[i : i + 1, :]

    def send(src, dst, phase, device):
        pltpu.make_async_remote_copy(
            src_ref=src, dst_ref=dst, send_sem=sends.at[phase], recv_sem=recvs.at[phase], device_id=device, device_id_type=MESH
        ).start()

    def segments(axis):
        return lax.broadcasted_iota(I32, (LANES, LANES), axis) // SEGMENT

    segment_sum = (segments(0) == segments(1)).astype(BF16)

    def lay(ref, where, *pairs):
        codes = None
        for p, pair in enumerate(pairs):
            for g in range(groups):
                first, second = (value[:, g * LANES : (g + 1) * LANES] for value in pair)
                square = jnp.dot(
                    (first * first + second * second).astype(BF16), segment_sum, preferred_element_type=F32
                )
                code = jnp.ceil(2.0 * jnp.log2(jnp.maximum(square, 1e-36) * 1.02))
                factor = TOP * jnp.exp2(code * -0.25)
                a = jnp.round(first * factor).astype(I32)
                b = jnp.round(second * factor).astype(I32)
                k = p * groups + g
                ref[where, k, 0, :] = (a << 16) | (b & 0xFFFF)
                within = lax.broadcasted_iota(I32, code.shape, 1) % SEGMENT
                codes = code if codes is None else jnp.where(within == k, code, codes)
        ref[where, len(pairs) * groups, 0, :] = codes.astype(I32)

    def lift(ref, where, pairs=2):
        codes = ref[where, pairs * groups, 0, :].astype(F32)
        within = lax.broadcasted_iota(I32, codes.shape, 1) % SEGMENT
        values = []
        for p in range(pairs):
            firsts, seconds = [], []
            for g in range(groups):
                k = p * groups + g
                code = jnp.dot(
                    jnp.where(within == k, codes, 0.0).astype(BF16), segment_sum, preferred_element_type=F32
                )
                scale = jnp.exp2(code * 0.25) * (1.0 / TOP)
                words = ref[where, k, 0, :]
                firsts.append((words >> 16).astype(F32) * scale)
                seconds.append(((words << 16) >> 16).astype(F32) * scale)
            values.append((jnp.concatenate(firsts, axis=1), jnp.concatenate(seconds, axis=1)))
        return values

    def block_moments(ref, h):
        rate = line(0)
        onward = rate * at(ref, h, 0)
        backward = rate * at(ref, h, cells - 1)
        for i in range(1, cells):
            onward = (onward + at(ref, h, i)) * rate
            backward = (backward + at(ref, h, cells - 1 - i)) * rate
        return onward, backward

    def finish(ref, h, left=None, right=None):
        rate = line(0)
        running = right
        for i in range(cells - 1, -1, -1):
            if running is not None:
                result[h, i * half : (i + 1) * half, :] = running
            running = (at(ref, h, i) if running is None else running + at(ref, h, i)) * rate
        running = left
        for i in range(cells):
            value = at(ref, h, i)
            running = value if running is None else value + (running if i == 0 else running * rate)
            full = running if right is None and i == cells - 1 else running + at(result, h, i)
            split(h, i, full * line(2))
        result[h] = sine(h)

    def misfit(h, keep):
        chosen = lax.broadcasted_iota(I32, (half, planes), 0) + h * half == lax.broadcasted_iota(I32, (half, planes), 1)
        first_row = jnp.sum(jnp.where(chosen, walls[...], 0), axis=1, keepdims=True)
        outside = lax.broadcasted_iota(I32, (half, rows), 1) >= first_row
        for i in range(cells):
            value = at(result, h, i)
            if keep:
                pressure[lines(h, i), :] = value
            split(h, i, jnp.where(outside, value - measured[lines(h, i), :].astype(F32), 0.0))

    around = [(step, y) for step in (1, 0) for y in (2, 1, 3, 0)]

    def give(h, far):
        for i in range(cells):
            value = viscosity[lines(h, i), :].astype(F32) * at(result, h, i)
            put(rs_send.at[h * cells + i], value[: half // 2], value[half // 2 :])
        for step, y in around if far else around[:-1]:
            other = case_at(far, step, y)
            send(rs_send.at[other], rs_got.at[case], 2, {"case": other})

    for i in range(3):
        loads[i].wait()
    for h in range(2):
        for i in range(cells):
            part = lines(h, i)
            split(h, i, forcing[part, :].astype(F32) + viscosity[part, :].astype(F32) * correction[part, :])
    for i in range(3, 8):
        loads[i].wait()
    walls_send[...] = jnp.zeros_like(walls_send)
    walls_send[:, 0:planes] = walls[...]
    for h in range(2):
        some = slice(h * half, (h + 1) * half)
        spectrum[h] = sine(h)
        field = block_moments(spectrum, h)
        finish(spectrum, h)
        misfit(h, False)
        result[h] = sine(h)
        lay(a_send, some, field, block_moments(result, h))
    pl.semaphore_wait(barrier, cases - 1 + spaces)
    send(walls_send, walls_got, 4, solver(me))
    for o, m, i in nearby((1, 2, 3, 0)):
        plane = place(o, m, i)
        send(a_send.at[plane], a_got.at[me], 0, solver(plane))

    wait_bytes(walls_got, recvs.at[4])
    chosen = lax.broadcasted_iota(I32, walls_got.shape, 1) == owned
    first_row = jnp.sum(jnp.where(chosen, walls_got[...], 0), axis=1, keepdims=True)
    outside = lax.broadcasted_iota(I32, (1, rows), 1) >= first_row
    wait_bytes(a_got, recvs.at[0])
    every = slice(0, spaces)

    def scan(onward, backward):
        step, k = 1, 3
        while step < spaces:
            onward = onward + line(k) * pltpu.roll(onward, step, 0)
            backward = backward + line(k) * pltpu.roll(backward, spaces - step, 0)
            step, k = 2 * step, k + 1
        return pltpu.roll(onward, 1, 0) * line(1), pltpu.roll(backward, spaces - 1, 0) * line(1)

    rate = line(0)
    field, alone = lift(a_got, every)
    left, right = scan(*field)
    quarter = cells // 2
    powers = [line(2)]
    for i in range(1, cells):
        powers.append(powers[-1] * rate)
    for i in range(cells):
        split(i // quarter, i % quarter, left * powers[i] + right * powers[cells - 1 - i])

    def row_block(i):
        return result[i // quarter, (i % quarter) * spaces : (i % quarter + 1) * spaces, :]

    for h in range(2):
        result[h] = sine(h)
    for i in range(cells):
        split(i // quarter, i % quarter, jnp.where(outside, row_block(i), 0.0))
    for h in range(2):
        result[h] = sine(h)
    onward, backward = rate * row_block(0), rate * row_block(cells - 1)
    for i in range(1, cells):
        onward = (onward + row_block(i)) * rate
        backward = (backward + row_block(cells - 1 - i)) * rate
    lay(b_send, every, (left, right), scan(alone[0] + onward, alone[1] + backward))
    for o, m, i in nearby((1, 2, 3, 0)):
        target = place(o, m + upper_case, i)
        send(b_send.at[target], b_got.at[owned], 1, {"case": partner, "space": target})
    wait_bytes(b_got, recvs.at[1])

    for far in (1, 0):
        h = (upper_case + far) % 2
        some = pl.ds(h * half, half)
        first, second = lift(b_got, some)
        finish(spectrum, h, *first)
        misfit(h, True)
        spectrum[h] = sine(h)
        finish(spectrum, h, *second)
        give(h, far)
    copy_out = pltpu.make_async_copy(pressure, pressure_out, out_sems.at[0])
    copy_out.start()
    rs_got[case] = rs_send[case]
    wait_bytes(a_got, sends.at[0])
    wait_bytes(b_got, sends.at[1])
    wait_bytes(walls_got, sends.at[4])
    wait_bytes(rs_got.at[pl.ds(0, cases - 1)], recvs.at[2])
    upper, lower = take(rs_got.at[0], groups)
    for k in range(1, cases):
        a, b = take(rs_got.at[k], groups)
        upper, lower = upper + a, lower + b
    put(ag_send, upper, lower)
    for far in (1, 0):
        for step, y in around if far else around[:-1]:
            send(ag_send, words_out.at[case], 3, {"case": case_at(far, step, y)})
    keep = pltpu.make_async_copy(ag_send, words_out.at[case], out_sems.at[1])
    keep.start()
    wait_bytes(rs_got.at[pl.ds(0, cases - 1)], sends.at[2])
    copy_out.wait()
    keep.wait()
    wait_bytes(words_out.at[pl.ds(0, cases - 1)], recvs.at[3])
    wait_bytes(words_out.at[pl.ds(0, cases - 1)], sends.at[3])


def spread(cells, planes, pressure_in, words, pressure_out, gradient_out, gradient, sems):
    copies = [pltpu.make_async_copy(pressure_in, pressure_out, sems.at[0])]
    copies[0].start()
    half = planes // 2
    for h in range(2):
        for i in range(cells):
            a, b = take(words.at[h * cells + i], gradient.shape[1] // LANES)
            start = i * planes + h * half
            gradient[start : start + half // 2, :] = a
            gradient[start + half // 2 : start + half, :] = b
    copies.append(pltpu.make_async_copy(gradient, gradient_out, sems.at[1]))
    copies[1].start()
    for copy in copies:
        copy.wait()


def shards(forcing, viscosity, measured, correction, wall_rows):
    cells, planes, rows = correction.shape
    spaces, cases = lax.axis_size("space"), lax.axis_size("case")
    assert spaces == 2 * OUTER * MIDDLE and cases == 2 * cells
    high, low = sine_tables(rows)
    modes = mode_table(rows, cells, cells * spaces, 1.0 / (2.0 * cells))
    flat = (cells * planes, rows)
    half, groups = planes // 2, rows // LANES
    halves = (2, cells * half, rows)
    short = (groups * (half // 2 + 1), LANES)
    there = pl.BlockSpec(memory_space=pltpu.HBM)
    anywhere = pl.BlockSpec(memory_space=pl.ANY)
    pressure, words = pl.pallas_call(
        functools.partial(kernel, cases, cells, planes, rows),
        out_shape=(jax.ShapeDtypeStruct(flat, F32), jax.ShapeDtypeStruct((cases, *short), I32)),
        in_specs=[there] * 8,
        out_specs=(anywhere,) * 2,
        scratch_shapes=[
            pltpu.VMEM(flat, BF16),
            pltpu.VMEM(flat, BF16),
            pltpu.VMEM(flat, BF16),
            pltpu.VMEM(flat, F32),
            pltpu.VMEM((1, planes), I32),
            pltpu.VMEM((rows, rows), BF16),
            pltpu.VMEM((rows, rows), BF16),
            pltpu.VMEM(modes.shape, F32),
            pltpu.VMEM(halves, BF16),
            pltpu.VMEM(halves, BF16),
            pltpu.VMEM(halves, F32),
            pltpu.VMEM(halves, F32),
            pltpu.VMEM(flat, F32),
            pltpu.VMEM((1, LANES), I32),
            pltpu.VMEM((1, LANES), I32),
            *[pltpu.VMEM((spaces, 2 * groups + 1, 1, LANES), I32)] * 4,
            pltpu.VMEM((cases, *short), I32),
            pltpu.VMEM((cases, *short), I32),
            pltpu.VMEM(short, I32),
            pltpu.SemaphoreType.DMA((8,)),
            pltpu.SemaphoreType.DMA((2,)),
            pltpu.SemaphoreType.DMA((5,)),
            pltpu.SemaphoreType.DMA((5,)),
        ],
        compiler_params=pltpu.CompilerParams(
            collective_id=0, has_side_effects=True, vmem_limit_bytes=LIMIT * 1024 * 1024
        ),
    )(
        *(pltpu.with_memory_space_constraint(x, pltpu.HBM) for x in (forcing.reshape(flat),
        viscosity.reshape(flat),
        measured.reshape(flat),
        correction.reshape(flat),
        wall_rows,
        jnp.asarray(high),
        jnp.asarray(low),
        jnp.asarray(modes))),
    )
    pressure, gradient = pl.pallas_call(
        functools.partial(spread, cells, planes),
        out_shape=(jax.ShapeDtypeStruct(flat, F32), jax.ShapeDtypeStruct(flat, F32)),
        in_specs=[anywhere, pl.BlockSpec(memory_space=pltpu.VMEM)],
        out_specs=(anywhere,) * 2,
        scratch_shapes=[pltpu.VMEM(flat, F32), pltpu.SemaphoreType.DMA((2,))],
        compiler_params=pltpu.CompilerParams(vmem_limit_bytes=LIMIT * 1024 * 1024),
    )(pressure, words)
    return pressure.reshape(forcing.shape), gradient.reshape(correction.shape)


def solution(mesh):
    return jax.shard_map(
        shards,
        mesh=mesh,
        in_specs=(
            P("case", "space", None, None),
            P("case", "space", None, None),
            P("case", "space", None, None),
            P("space", None, None),
            P("case", None),
        ),
        out_specs=(P("case", "space", None, None), P("space", None, None)),
        check_vma=False,
    )
```

```python
import functools

import jax
import jax.numpy as jnp
import ml_dtypes
import numpy as np
from jax import lax
from jax.experimental import pallas as pl
from jax.experimental.pallas import tpu as pltpu
from jax.sharding import PartitionSpec as P

MESH = pl.DeviceIdType.MESH
F32, BF16, I32 = jnp.float32, jnp.bfloat16, jnp.int32
OUTER, MIDDLE = 4, 4
TOP = 32767.0
LANES = 128
SEGMENT = 16
LIMIT = 16


def sine_tables(rows):
    index = np.arange(1, rows + 1, dtype=np.float64)
    phase = (index[:, None] * index[None, :]) % (2 * (rows + 1))
    sine = np.sqrt(2.0 / (rows + 1)) * np.sin(np.pi * phase / (rows + 1))
    high = sine.astype(ml_dtypes.bfloat16)
    low = (sine - high.astype(np.float64)).astype(ml_dtypes.bfloat16)
    return high, low


def mode_table(rows, cells, length, screen):
    index = np.arange(1, rows + 1, dtype=np.float64)
    centre = 4.0 * np.sin(np.pi * index / (2 * (rows + 1))) ** 2 + screen * screen
    rate = 1.0 + centre / 2.0 - np.sqrt(centre + centre * centre / 4.0)
    lines = [rate, 1.0 / (1.0 - rate**length), screen / (1.0 / rate - rate)]
    step = 1
    while step < length // cells:
        lines.append(rate ** (cells * step))
        step *= 2
    table = np.zeros((-(-len(lines) // 8) * 8, rows))
    table[: len(lines)] = lines
    return table.astype(np.float32)


def wait_bytes(ref, sem):
    pltpu.make_async_copy(ref, ref, sem).wait()


def pack(first, second):
    largest = jnp.max(jnp.maximum(jnp.abs(first), jnp.abs(second)), axis=0, keepdims=True)
    code = jnp.ceil(jnp.log2(jnp.maximum(largest, 1e-30)) * 64.0)
    factor = TOP * jnp.exp2(code * (-1.0 / 64.0))
    a = jnp.round(first * factor).astype(I32)
    b = jnp.round(second * factor).astype(I32)
    return (a << 16) | (b & 0xFFFF), code.astype(I32)


def put(ref, first, second):
    words, code = pack(first, second)
    count, groups = words.shape[0], words.shape[1] // LANES
    for g in range(groups):
        ref[g * count : (g + 1) * count, :] = words[:, g * LANES : (g + 1) * LANES]
        ref[groups * count + g : groups * count + g + 1, :] = code[:, g * LANES : (g + 1) * LANES]


def take(ref, groups):
    count = ref.shape[0] // groups - 1
    first, second = [], []
    for g in range(groups):
        code = ref[groups * count + g : groups * count + g + 1, :]
        scale = jnp.exp2(code.astype(F32) * (1.0 / 64.0)) * (1.0 / TOP)
        words = ref[g * count : (g + 1) * count, :]
        first.append((words >> 16).astype(F32) * scale)
        second.append(((words << 16) >> 16).astype(F32) * scale)
    return jnp.concatenate(first, axis=1), jnp.concatenate(second, axis=1)


def kernel(cases, cells, planes, rows, forcing_in, viscosity_in, measured_in, correction_in, walls_in, high_in, low_in,
           modes_in, pressure_out, words_out, forcing, viscosity, measured, correction, walls, high_ref, low_ref, modes,
           head, tail, spectrum, result, pressure, walls_send, walls_got, a_send, a_got, b_send, b_got,
           rs_send, rs_got, ag_send, in_sems, out_sems, sends, recvs):
    me = lax.axis_index("space")
    case = lax.axis_index("case")
    inner, middle, outer = me & 1, (me >> 1) & (MIDDLE - 1), lax.div(me, 2 * MIDDLE)
    half = planes // 2
    groups = rows // LANES
    spaces = 2 * OUTER * MIDDLE
    partner = lax.rem(case + cases // 2, cases)
    upper_case = lax.div(case, cases // 2)
    owned = (outer * MIDDLE + ((middle + MIDDLE - 1 + upper_case) & (MIDDLE - 1))) * 2 + inner

    def nearby(steps):
        return [(o, m, i) for m in steps for o in (2, 1, 3, 0) for i in (1, 0)]

    barrier = pltpu.get_barrier_semaphore()

    def greet(device):
        pl.semaphore_signal(barrier, inc=1, device_id=device, device_id_type=MESH)

    outers = [((outer + k) & (OUTER - 1)) * (2 * MIDDLE) for k in range(OUTER)]
    middles = [((middle + k) & (MIDDLE - 1)) * 2 for k in range(MIDDLE)]
    others = [((middle + k + upper_case) & (MIDDLE - 1)) * 2 for k in range(MIDDLE)]
    inners = [inner, 1 - inner]

    def place(o, m, i):
        return outers[o] + middles[m] + inners[i]

    def across(o, m, i):
        return outers[o] + others[m] + inners[i]

    loads = [
        pltpu.make_async_copy(src, dst, in_sems.at[i])
        for i, (src, dst) in enumerate(
            (
                (forcing_in, forcing),
                (viscosity_in, viscosity),
                (correction_in, correction),
                (high_in, high_ref),
                (low_in, low_ref),
                (modes_in, modes),
                (walls_in, walls),
                (measured_in, measured),
            )
        )
    ]
    for load in loads[:3]:
        load.start()
    for o, m, i in nearby((1, 2, 3, 0)):
        greet({"case": partner, "space": across(o, m, i)})
    for load in loads[3:]:
        load.start()
    for k in range(1, cases):
        greet({"case": lax.rem(case + k, cases)})

    def lines(h, i):
        return pl.ds(pl.multiple_of(i * planes + h * half, half), half)

    halves = [upper_case, 1 - upper_case]
    lower_bit = lax.div(case, 4) & 1
    bits = [lower_bit * 4, 4 - lower_bit * 4]
    columns = [(case + k) & 3 for k in range(4)]

    def case_at(far, step, y):
        return halves[far] * (cases // 2) + bits[step] + columns[y]

    def split(h, i, value):
        count = value.shape[0]
        top = value.astype(BF16)
        head[h, i * count : (i + 1) * count, :] = top
        tail[h, i * count : (i + 1) * count, :] = (value - top.astype(F32)).astype(BF16)

    def sine(h):
        high, low = high_ref[...], low_ref[...]
        top = head[h]
        small = jnp.dot(top, low, preferred_element_type=F32) + jnp.dot(tail[h], high, preferred_element_type=F32)
        return jnp.dot(top, high, preferred_element_type=F32) + small

    def at(ref, h, i):
        return ref[h, i * half : (i + 1) * half, :]

    def line(i):
        return modes[i : i + 1, :]

    def send(src, dst, phase, device):
        pltpu.make_async_remote_copy(
            src_ref=src, dst_ref=dst, send_sem=sends.at[phase], recv_sem=recvs.at[phase], device_id=device, device_id_type=MESH
        ).start()

    def segments(axis):
        return lax.broadcasted_iota(I32, (LANES, LANES), axis) // SEGMENT

    segment_sum = (segments(0) == segments(1)).astype(BF16)

    def lay(ref, where, *pairs):
        codes = None
        for p, pair in enumerate(pairs):
            for g in range(groups):
                first, second = (value[:, g * LANES : (g + 1) * LANES] for value in pair)
                square = jnp.dot(
                    (first * first + second * second).astype(BF16), segment_sum, preferred_element_type=F32
                )
                code = jnp.ceil(2.0 * jnp.log2(jnp.maximum(square, 1e-36) * 1.02))
                factor = TOP * jnp.exp2(code * -0.25)
                a = jnp.round(first * factor).astype(I32)
                b = jnp.round(second * factor).astype(I32)
                k = p * groups + g
                ref[where, k, 0, :] = (a << 16) | (b & 0xFFFF)
                within = lax.broadcasted_iota(I32, code.shape, 1) % SEGMENT
                codes = code if codes is None else jnp.where(within == k, code, codes)
        ref[where, len(pairs) * groups, 0, :] = codes.astype(I32)

    def lift(ref, where, pairs=2):
        codes = ref[where, pairs * groups, 0, :].astype(F32)
        within = lax.broadcasted_iota(I32, codes.shape, 1) % SEGMENT
        values = []
        for p in range(pairs):
            firsts, seconds = [], []
            for g in range(groups):
                k = p * groups + g
                code = jnp.dot(
                    jnp.where(within == k, codes, 0.0).astype(BF16), segment_sum, preferred_element_type=F32
                )
                scale = jnp.exp2(code * 0.25) * (1.0 / TOP)
                words = ref[where, k, 0, :]
                firsts.append((words >> 16).astype(F32) * scale)
                seconds.append(((words << 16) >> 16).astype(F32) * scale)
            values.append((jnp.concatenate(firsts, axis=1), jnp.concatenate(seconds, axis=1)))
        return values

    def block_moments(ref, h):
        rate = line(0)
        onward = rate * at(ref, h, 0)
        backward = rate * at(ref, h, cells - 1)
        for i in range(1, cells):
            onward = (onward + at(ref, h, i)) * rate
            backward = (backward + at(ref, h, cells - 1 - i)) * rate
        return onward, backward

    def finish(ref, h, left=None, right=None):
        rate = line(0)
        running = right
        for i in range(cells - 1, -1, -1):
            if running is not None:
                result[h, i * half : (i + 1) * half, :] = running
            running = (at(ref, h, i) if running is None else running + at(ref, h, i)) * rate
        running = left
        for i in range(cells):
            value = at(ref, h, i)
            running = value if running is None else value + (running if i == 0 else running * rate)
            full = running if right is None and i == cells - 1 else running + at(result, h, i)
            split(h, i, full * line(2))
        result[h] = sine(h)

    def misfit(f, h, keep):
        chosen = lax.broadcasted_iota(I32, (half, planes), 0) + h * half == lax.broadcasted_iota(I32, (half, planes), 1)
        first_row = jnp.sum(jnp.where(chosen, walls[...], 0), axis=1, keepdims=True)
        outside = lax.broadcasted_iota(I32, (half, rows), 1) >= first_row
        for i in range(cells):
            value = at(result, f, i)
            if keep:
                pressure[lines(h, i), :] = value
            split(f, i, jnp.where(outside, value - measured[lines(h, i), :].astype(F32), 0.0))

    around = [(step, y) for step in (1, 0) for y in (2, 1, 3, 0)]

    def give(f, h, far):
        for i in range(cells):
            value = viscosity[lines(h, i), :].astype(F32) * at(result, f, i)
            put(rs_send.at[h * cells + i], value[: half // 2], value[half // 2 :])
        for step, y in around if far else around[:-1]:
            other = case_at(far, step, y)
            send(rs_send.at[other], rs_got.at[case], 2, {"case": other})

    for i in range(3):
        loads[i].wait()
    for f in range(2):
        for i in range(cells):
            part = lines(halves[1 - f], i)
            split(f, i, forcing[part, :].astype(F32) + viscosity[part, :].astype(F32) * correction[part, :])
    for i in range(3, 8):
        loads[i].wait()
    walls_send[...] = jnp.zeros_like(walls_send)
    walls_send[:, 0:planes] = walls[...]
    for f in range(2):
        h = halves[1 - f]
        spectrum[f] = sine(f)
        field = block_moments(spectrum, f)
        finish(spectrum, f)
        misfit(f, h, False)
        result[f] = sine(f)
        lay(a_send, pl.ds(h * half, half), field, block_moments(result, f))
    pl.semaphore_wait(barrier, cases - 1 + spaces)
    send(walls_send, walls_got, 4, {"case": partner, "space": across(0, 0, 0)})
    for o, m, i in nearby((1, 2, 3, 0)):
        plane = place(o, m, i)
        send(a_send.at[plane], a_got.at[me], 0, {"case": partner, "space": across(o, m, i)})

    wait_bytes(walls_got, recvs.at[4])
    chosen = lax.broadcasted_iota(I32, walls_got.shape, 1) == owned
    first_row = jnp.sum(jnp.where(chosen, walls_got[...], 0), axis=1, keepdims=True)
    outside = lax.broadcasted_iota(I32, (1, rows), 1) >= first_row
    wait_bytes(a_got, recvs.at[0])
    every = slice(0, spaces)

    def scan(onward, backward):
        step, k = 1, 3
        while step < spaces:
            onward = onward + line(k) * pltpu.roll(onward, step, 0)
            backward = backward + line(k) * pltpu.roll(backward, spaces - step, 0)
            step, k = 2 * step, k + 1
        return pltpu.roll(onward, 1, 0) * line(1), pltpu.roll(backward, spaces - 1, 0) * line(1)

    rate = line(0)
    field, alone = lift(a_got, every)
    left, right = scan(*field)
    quarter = cells // 2
    powers = [line(2)]
    for i in range(1, cells):
        powers.append(powers[-1] * rate)
    for i in range(cells):
        split(i // quarter, i % quarter, left * powers[i] + right * powers[cells - 1 - i])

    def row_block(i):
        return result[i // quarter, (i % quarter) * spaces : (i % quarter + 1) * spaces, :]

    for h in range(2):
        result[h] = sine(h)
    for i in range(cells):
        split(i // quarter, i % quarter, jnp.where(outside, row_block(i), 0.0))
    for h in range(2):
        result[h] = sine(h)
    onward, backward = rate * row_block(0), rate * row_block(cells - 1)
    for i in range(1, cells):
        onward = (onward + row_block(i)) * rate
        backward = (backward + row_block(cells - 1 - i)) * rate
    lay(b_send, every, (left, right), scan(alone[0] + onward, alone[1] + backward))
    for o, m, i in nearby((1, 2, 3, 0)):
        target = across(o, m, i)
        send(b_send.at[target], b_got.at[owned], 1, {"case": partner, "space": target})
    wait_bytes(b_got, recvs.at[1])

    rows_back = [lift(b_got, pl.ds(halves[1 - f] * half, half)) for f in range(2)]
    for f in range(2):
        finish(spectrum, f, *rows_back[f][0])
    for f in range(2):
        misfit(f, halves[1 - f], True)
    for f in range(2):
        spectrum[f] = sine(f)
    for f in range(2):
        finish(spectrum, f, *rows_back[f][1])
    for f in range(2):
        give(f, halves[1 - f], 1 - f)
    copy_out = pltpu.make_async_copy(pressure, pressure_out, out_sems.at[0])
    copy_out.start()
    rs_got[case] = rs_send[case]
    wait_bytes(a_got, sends.at[0])
    wait_bytes(b_got, sends.at[1])
    wait_bytes(walls_got, sends.at[4])
    wait_bytes(rs_got.at[pl.ds(0, cases - 1)], recvs.at[2])
    upper, lower = take(rs_got.at[0], groups)
    for k in range(1, cases):
        a, b = take(rs_got.at[k], groups)
        upper, lower = upper + a, lower + b
    put(ag_send, upper, lower)
    for far in (1, 0):
        for step, y in around if far else around[:-1]:
            send(ag_send, words_out.at[case], 3, {"case": case_at(far, step, y)})
    keep = pltpu.make_async_copy(ag_send, words_out.at[case], out_sems.at[1])
    keep.start()
    wait_bytes(rs_got.at[pl.ds(0, cases - 1)], sends.at[2])
    copy_out.wait()
    keep.wait()
    wait_bytes(words_out.at[pl.ds(0, cases - 1)], recvs.at[3])
    wait_bytes(words_out.at[pl.ds(0, cases - 1)], sends.at[3])


def spread(cells, planes, pressure_in, words, pressure_out, gradient_out, gradient, sems):
    copies = [pltpu.make_async_copy(pressure_in, pressure_out, sems.at[0])]
    copies[0].start()
    half = planes // 2
    for h in range(2):
        for i in range(cells):
            a, b = take(words.at[h * cells + i], gradient.shape[1] // LANES)
            start = i * planes + h * half
            gradient[start : start + half // 2, :] = a
            gradient[start + half // 2 : start + half, :] = b
    copies.append(pltpu.make_async_copy(gradient, gradient_out, sems.at[1]))
    copies[1].start()
    for copy in copies:
        copy.wait()


def shards(forcing, viscosity, measured, correction, wall_rows):
    cells, planes, rows = correction.shape
    spaces, cases = lax.axis_size("space"), lax.axis_size("case")
    assert spaces == 2 * OUTER * MIDDLE and cases == 2 * cells == 16
    high, low = sine_tables(rows)
    modes = mode_table(rows, cells, cells * spaces, 1.0 / (2.0 * cells))
    flat = (cells * planes, rows)
    half, groups = planes // 2, rows // LANES
    halves = (2, cells * half, rows)
    short = (groups * (half // 2 + 1), LANES)
    there = pl.BlockSpec(memory_space=pltpu.HBM)
    anywhere = pl.BlockSpec(memory_space=pl.ANY)
    pressure, words = pl.pallas_call(
        functools.partial(kernel, cases, cells, planes, rows),
        out_shape=(jax.ShapeDtypeStruct(flat, F32), jax.ShapeDtypeStruct((cases, *short), I32)),
        in_specs=[there] * 8,
        out_specs=(anywhere,) * 2,
        scratch_shapes=[
            pltpu.VMEM(flat, BF16),
            pltpu.VMEM(flat, BF16),
            pltpu.VMEM(flat, BF16),
            pltpu.VMEM(flat, F32),
            pltpu.VMEM((1, planes), I32),
            pltpu.VMEM((rows, rows), BF16),
            pltpu.VMEM((rows, rows), BF16),
            pltpu.VMEM(modes.shape, F32),
            pltpu.VMEM(halves, BF16),
            pltpu.VMEM(halves, BF16),
            pltpu.VMEM(halves, F32),
            pltpu.VMEM(halves, F32),
            pltpu.VMEM(flat, F32),
            pltpu.VMEM((1, LANES), I32),
            pltpu.VMEM((1, LANES), I32),
            *[pltpu.VMEM((spaces, 2 * groups + 1, 1, LANES), I32)] * 4,
            pltpu.VMEM((cases, *short), I32),
            pltpu.VMEM((cases, *short), I32),
            pltpu.VMEM(short, I32),
            pltpu.SemaphoreType.DMA((8,)),
            pltpu.SemaphoreType.DMA((2,)),
            pltpu.SemaphoreType.DMA((5,)),
            pltpu.SemaphoreType.DMA((5,)),
        ],
        compiler_params=pltpu.CompilerParams(
            collective_id=0, has_side_effects=True, vmem_limit_bytes=LIMIT * 1024 * 1024
        ),
    )(
        *(pltpu.with_memory_space_constraint(x, pltpu.HBM) for x in (forcing.reshape(flat),
        viscosity.reshape(flat),
        measured.reshape(flat),
        correction.reshape(flat),
        wall_rows,
        jnp.asarray(high),
        jnp.asarray(low),
        jnp.asarray(modes))),
    )
    pressure, gradient = pl.pallas_call(
        functools.partial(spread, cells, planes),
        out_shape=(jax.ShapeDtypeStruct(flat, F32), jax.ShapeDtypeStruct(flat, F32)),
        in_specs=[anywhere, pl.BlockSpec(memory_space=pltpu.VMEM)],
        out_specs=(anywhere,) * 2,
        scratch_shapes=[pltpu.VMEM(flat, F32), pltpu.SemaphoreType.DMA((2,))],
        compiler_params=pltpu.CompilerParams(vmem_limit_bytes=LIMIT * 1024 * 1024),
    )(pressure, words)
    return pressure.reshape(forcing.shape), gradient.reshape(correction.shape)


def solution(mesh):
    return jax.shard_map(
        shards,
        mesh=mesh,
        in_specs=(
            P("case", "space", None, None),
            P("case", "space", None, None),
            P("case", "space", None, None),
            P("space", None, None),
            P("case", None),
        ),
        out_specs=(P("case", "space", None, None), P("space", None, None)),
        check_vma=False,
    )
```

```python
import functools

import jax
import jax.numpy as jnp
import ml_dtypes
import numpy as np
from jax import lax
from jax.experimental import pallas as pl
from jax.experimental.pallas import tpu as pltpu
from jax.sharding import PartitionSpec as P

MESH = pl.DeviceIdType.MESH
F32, BF16, I32 = jnp.float32, jnp.bfloat16, jnp.int32
OUTER, MIDDLE = 4, 4
TOP = 32767.0
LANES = 128
SEGMENT = 16
LIMIT = 16


def sine_tables(rows):
    index = np.arange(1, rows + 1, dtype=np.float64)
    phase = (index[:, None] * index[None, :]) % (2 * (rows + 1))
    sine = np.sqrt(2.0 / (rows + 1)) * np.sin(np.pi * phase / (rows + 1))
    high = sine.astype(ml_dtypes.bfloat16)
    low = (sine - high.astype(np.float64)).astype(ml_dtypes.bfloat16)
    return high, low


def mode_table(rows, cells, length, screen):
    index = np.arange(1, rows + 1, dtype=np.float64)
    centre = 4.0 * np.sin(np.pi * index / (2 * (rows + 1))) ** 2 + screen * screen
    rate = 1.0 + centre / 2.0 - np.sqrt(centre + centre * centre / 4.0)
    lines = [rate, 1.0 / (1.0 - rate**length), screen / (1.0 / rate - rate)]
    step = 1
    while step < length // cells:
        lines.append(rate ** (cells * step))
        step *= 2
    table = np.zeros((-(-len(lines) // 8) * 8, rows))
    table[: len(lines)] = lines
    return table.astype(np.float32)


def wait_bytes(ref, sem):
    pltpu.make_async_copy(ref, ref, sem).wait()


def pack(first, second):
    largest = jnp.max(jnp.maximum(jnp.abs(first), jnp.abs(second)), axis=0, keepdims=True)
    code = jnp.ceil(jnp.log2(jnp.maximum(largest, 1e-30)) * 64.0)
    factor = TOP * jnp.exp2(code * (-1.0 / 64.0))
    a = jnp.round(first * factor).astype(I32)
    b = jnp.round(second * factor).astype(I32)
    return (a << 16) | (b & 0xFFFF), code.astype(I32)


def put(ref, first, second):
    words, code = pack(first, second)
    count, groups = words.shape[0], words.shape[1] // LANES
    for g in range(groups):
        ref[g * count : (g + 1) * count, :] = words[:, g * LANES : (g + 1) * LANES]
        ref[groups * count + g : groups * count + g + 1, :] = code[:, g * LANES : (g + 1) * LANES]


def take(ref, groups):
    count = ref.shape[0] // groups - 1
    first, second = [], []
    for g in range(groups):
        code = ref[groups * count + g : groups * count + g + 1, :]
        scale = jnp.exp2(code.astype(F32) * (1.0 / 64.0)) * (1.0 / TOP)
        words = ref[g * count : (g + 1) * count, :]
        first.append((words >> 16).astype(F32) * scale)
        second.append(((words << 16) >> 16).astype(F32) * scale)
    return jnp.concatenate(first, axis=1), jnp.concatenate(second, axis=1)


def kernel(cases, cells, planes, rows, forcing_in, viscosity_in, measured_in, correction_in, walls_in, high_in, low_in,
           modes_in, pressure_out, words_out, forcing, viscosity, measured, correction, walls, high_ref, low_ref, modes,
           head, tail, spectrum, result, pressure, walls_send, walls_got, a_send, a_got, b_send, b_got,
           rs_send, rs_got, ag_send, in_sems, out_sems, sends, recvs):
    me = lax.axis_index("space")
    case = lax.axis_index("case")
    inner, middle, outer = me % 2, me // 2 % MIDDLE, me // (2 * MIDDLE)
    half = planes // 2
    groups = rows // LANES
    spaces = 2 * OUTER * MIDDLE
    partner = (case + cases // 2) % cases
    upper_case = case // (cases // 2)
    owned = (outer * MIDDLE + (middle + MIDDLE - 1 + upper_case) % MIDDLE) * 2 + inner

    def solver(plane):
        o, m, i = plane // (2 * MIDDLE), plane // 2 % MIDDLE, plane % 2
        return {"case": partner, "space": (o * MIDDLE + (m + upper_case) % MIDDLE) * 2 + i}

    def nearby(steps):
        return [(o, m, i) for m in steps for o in (2, 1, 3, 0) for i in (1, 0)]

    barrier = pltpu.get_barrier_semaphore()

    def greet(device):
        pl.semaphore_signal(barrier, inc=1, device_id=device, device_id_type=MESH)

    def place(o, m, i):
        return (((outer + o) % OUTER) * MIDDLE + (middle + m) % MIDDLE) * 2 + (inner + i) % 2

    loads = [
        pltpu.make_async_copy(src, dst, in_sems.at[i])
        for i, (src, dst) in enumerate(
            (
                (forcing_in, forcing),
                (viscosity_in, viscosity),
                (correction_in, correction),
                (high_in, high_ref),
                (low_in, low_ref),
                (modes_in, modes),
                (walls_in, walls),
                (measured_in, measured),
            )
        )
    ]
    for load in loads[:3]:
        load.start()
    for o, m, i in nearby((1, 2, 3, 0)):
        greet({"case": partner, "space": place(o, m + upper_case, i)})
    for load in loads[3:]:
        load.start()
    for k in range(1, cases):
        greet({"case": (case + k) % cases})

    def lines(h, i):
        return pl.ds(pl.multiple_of(i * planes + h * half, half), half)

    def case_at(far, step, y):
        bit = (case // 4 + step) % 2
        return (upper_case + far) % 2 * (cases // 2) + bit * 4 + (case + y) % 4

    def split(h, i, value):
        count = value.shape[0]
        top = value.astype(BF16)
        head[h, i * count : (i + 1) * count, :] = top
        tail[h, i * count : (i + 1) * count, :] = (value - top.astype(F32)).astype(BF16)

    def sine(h):
        high, low = high_ref[...], low_ref[...]
        top = head[h]
        small = jnp.dot(top, low, preferred_element_type=F32) + jnp.dot(tail[h], high, preferred_element_type=F32)
        return jnp.dot(top, high, preferred_element_type=F32) + small

    def at(ref, h, i):
        return ref[h, i * half : (i + 1) * half, :]

    def line(i):
        return modes[i : i + 1, :]

    def send(src, dst, phase, device):
        pltpu.make_async_remote_copy(
            src_ref=src, dst_ref=dst, send_sem=sends.at[phase], recv_sem=recvs.at[phase], device_id=device, device_id_type=MESH
        ).start()

    def segments(axis):
        return lax.broadcasted_iota(I32, (LANES, LANES), axis) // SEGMENT

    segment_sum = (segments(0) == segments(1)).astype(BF16)

    def lay(ref, where, *pairs, start=0, codes=None):
        for p, pair in enumerate(pairs, start):
            for g in range(groups):
                first, second = (value[:, g * LANES : (g + 1) * LANES] for value in pair)
                square = jnp.dot(
                    (first * first + second * second).astype(BF16), segment_sum, preferred_element_type=F32
                )
                code = jnp.ceil(2.0 * jnp.log2(jnp.maximum(square, 1e-36) * 1.02))
                factor = TOP * jnp.exp2(code * -0.25)
                a = jnp.round(first * factor).astype(I32)
                b = jnp.round(second * factor).astype(I32)
                k = p * groups + g
                ref[where, k, 0, :] = (a << 16) | (b & 0xFFFF)
                within = lax.broadcasted_iota(I32, code.shape, 1) % SEGMENT
                codes = code if codes is None else jnp.where(within == k, code, codes)
        if p == 1:
            ref[where, 2 * groups, 0, :] = codes.astype(I32)
        return codes

    def lift(ref, where, pairs=2):
        codes = ref[where, pairs * groups, 0, :].astype(F32)
        within = lax.broadcasted_iota(I32, codes.shape, 1) % SEGMENT
        values = []
        for p in range(pairs):
            firsts, seconds = [], []
            for g in range(groups):
                k = p * groups + g
                code = jnp.dot(
                    jnp.where(within == k, codes, 0.0).astype(BF16), segment_sum, preferred_element_type=F32
                )
                scale = jnp.exp2(code * 0.25) * (1.0 / TOP)
                words = ref[where, k, 0, :]
                firsts.append((words >> 16).astype(F32) * scale)
                seconds.append(((words << 16) >> 16).astype(F32) * scale)
            values.append((jnp.concatenate(firsts, axis=1), jnp.concatenate(seconds, axis=1)))
        return values

    def block_moments(ref, h):
        rate = line(0)
        onward = rate * at(ref, h, 0)
        backward = rate * at(ref, h, cells - 1)
        for i in range(1, cells):
            onward = (onward + at(ref, h, i)) * rate
            backward = (backward + at(ref, h, cells - 1 - i)) * rate
        return onward, backward

    def finish(ref, h, left=None, right=None):
        rate = line(0)
        running = right
        for i in range(cells - 1, -1, -1):
            if running is not None:
                result[h, i * half : (i + 1) * half, :] = running
            running = (at(ref, h, i) if running is None else running + at(ref, h, i)) * rate
        running = left
        for i in range(cells):
            value = at(ref, h, i)
            running = value if running is None else value + (running if i == 0 else running * rate)
            full = running if right is None and i == cells - 1 else running + at(result, h, i)
            split(h, i, full * line(2))
        result[h] = sine(h)

    def misfit(h, keep):
        chosen = lax.broadcasted_iota(I32, (half, planes), 0) + h * half == lax.broadcasted_iota(I32, (half, planes), 1)
        first_row = jnp.sum(jnp.where(chosen, walls[...], 0), axis=1, keepdims=True)
        outside = lax.broadcasted_iota(I32, (half, rows), 1) >= first_row
        for i in range(cells):
            value = at(result, h, i)
            if keep:
                pressure[lines(h, i), :] = value
            split(h, i, jnp.where(outside, value - measured[lines(h, i), :].astype(F32), 0.0))

    around = [(step, y) for step in (1, 0) for y in (2, 1, 3, 0)]

    def give(h, far):
        for i in range(cells):
            value = viscosity[lines(h, i), :].astype(F32) * at(result, h, i)
            put(rs_send.at[h * cells + i], value[: half // 2], value[half // 2 :])
        for step, y in around if far else around[:-1]:
            other = case_at(far, step, y)
            send(rs_send.at[other], rs_got.at[case], 2, {"case": other})

    for i in range(3):
        loads[i].wait()
    for h in range(2):
        for i in range(cells):
            part = lines(h, i)
            split(h, i, forcing[part, :].astype(F32) + viscosity[part, :].astype(F32) * correction[part, :])
    for i in range(3, 8):
        loads[i].wait()
    walls_send[...] = jnp.zeros_like(walls_send)
    walls_send[:, 0:planes] = walls[...]
    for h in range(2):
        some = slice(h * half, (h + 1) * half)
        spectrum[h] = sine(h)
        field = block_moments(spectrum, h)
        finish(spectrum, h)
        misfit(h, False)
        result[h] = sine(h)
        lay(a_send, some, field, block_moments(result, h))
    pl.semaphore_wait(barrier, cases - 1 + spaces)
    send(walls_send, walls_got, 4, solver(me))
    for o, m, i in nearby((1, 2, 3, 0)):
        plane = place(o, m, i)
        send(a_send.at[plane], a_got.at[me], 0, solver(plane))

    wait_bytes(walls_got, recvs.at[4])
    chosen = lax.broadcasted_iota(I32, walls_got.shape, 1) == owned
    first_row = jnp.sum(jnp.where(chosen, walls_got[...], 0), axis=1, keepdims=True)
    outside = lax.broadcasted_iota(I32, (1, rows), 1) >= first_row
    wait_bytes(a_got, recvs.at[0])
    every = slice(0, spaces)

    def scan(onward, backward):
        step, k = 1, 3
        while step < spaces:
            onward = onward + line(k) * pltpu.roll(onward, step, 0)
            backward = backward + line(k) * pltpu.roll(backward, spaces - step, 0)
            step, k = 2 * step, k + 1
        return pltpu.roll(onward, 1, 0) * line(1), pltpu.roll(backward, spaces - 1, 0) * line(1)

    rate = line(0)
    field, alone = lift(a_got, every)
    left, right = scan(*field)
    codes = lay(b_send, every, (left, right))
    quarter = cells // 2
    powers = [line(2)]
    for i in range(1, cells):
        powers.append(powers[-1] * rate)
    for i in range(cells):
        split(i // quarter, i % quarter, left * powers[i] + right * powers[cells - 1 - i])

    def row_block(i):
        return result[i // quarter, (i % quarter) * spaces : (i % quarter + 1) * spaces, :]

    for h in range(2):
        result[h] = sine(h)
    for i in range(cells):
        split(i // quarter, i % quarter, jnp.where(outside, row_block(i), 0.0))
    for h in range(2):
        result[h] = sine(h)
    onward, backward = rate * row_block(0), rate * row_block(cells - 1)
    for i in range(1, cells):
        onward = (onward + row_block(i)) * rate
        backward = (backward + row_block(cells - 1 - i)) * rate
    lay(b_send, every, scan(alone[0] + onward, alone[1] + backward), start=1, codes=codes)
    for o, m, i in nearby((1, 2, 3, 0)):
        target = place(o, m + upper_case, i)
        send(b_send.at[target], b_got.at[owned], 1, {"case": partner, "space": target})
    wait_bytes(b_got, recvs.at[1])

    for far in (1, 0):
        h = (upper_case + far) % 2
        some = pl.ds(h * half, half)
        first, second = lift(b_got, some)
        finish(spectrum, h, *first)
        misfit(h, True)
        spectrum[h] = sine(h)
        finish(spectrum, h, *second)
        give(h, far)
    copy_out = pltpu.make_async_copy(pressure, pressure_out, out_sems.at[0])
    copy_out.start()
    rs_got[case] = rs_send[case]
    wait_bytes(a_got, sends.at[0])
    wait_bytes(b_got, sends.at[1])
    wait_bytes(walls_got, sends.at[4])
    wait_bytes(rs_got.at[pl.ds(0, cases - 1)], recvs.at[2])
    upper, lower = take(rs_got.at[0], groups)
    for k in range(1, cases):
        a, b = take(rs_got.at[k], groups)
        upper, lower = upper + a, lower + b
    put(ag_send, upper, lower)
    for far in (1, 0):
        for step, y in around if far else around[:-1]:
            send(ag_send, words_out.at[case], 3, {"case": case_at(far, step, y)})
    keep = pltpu.make_async_copy(ag_send, words_out.at[case], out_sems.at[1])
    keep.start()
    wait_bytes(rs_got.at[pl.ds(0, cases - 1)], sends.at[2])
    copy_out.wait()
    keep.wait()
    wait_bytes(words_out.at[pl.ds(0, cases - 1)], recvs.at[3])
    wait_bytes(words_out.at[pl.ds(0, cases - 1)], sends.at[3])


def spread(cells, planes, pressure_in, words, pressure_out, gradient_out, gradient, sems):
    copies = [pltpu.make_async_copy(pressure_in, pressure_out, sems.at[0])]
    copies[0].start()
    half = planes // 2
    for h in range(2):
        for i in range(cells):
            a, b = take(words.at[h * cells + i], gradient.shape[1] // LANES)
            start = i * planes + h * half
            gradient[start : start + half // 2, :] = a
            gradient[start + half // 2 : start + half, :] = b
    copies.append(pltpu.make_async_copy(gradient, gradient_out, sems.at[1]))
    copies[1].start()
    for copy in copies:
        copy.wait()


def shards(forcing, viscosity, measured, correction, wall_rows):
    cells, planes, rows = correction.shape
    spaces, cases = lax.axis_size("space"), lax.axis_size("case")
    assert spaces == 2 * OUTER * MIDDLE and cases == 2 * cells
    high, low = sine_tables(rows)
    modes = mode_table(rows, cells, cells * spaces, 1.0 / (2.0 * cells))
    flat = (cells * planes, rows)
    half, groups = planes // 2, rows // LANES
    halves = (2, cells * half, rows)
    short = (groups * (half // 2 + 1), LANES)
    there = pl.BlockSpec(memory_space=pltpu.HBM)
    anywhere = pl.BlockSpec(memory_space=pl.ANY)
    pressure, words = pl.pallas_call(
        functools.partial(kernel, cases, cells, planes, rows),
        out_shape=(jax.ShapeDtypeStruct(flat, F32), jax.ShapeDtypeStruct((cases, *short), I32)),
        in_specs=[there] * 8,
        out_specs=(anywhere,) * 2,
        scratch_shapes=[
            pltpu.VMEM(flat, BF16),
            pltpu.VMEM(flat, BF16),
            pltpu.VMEM(flat, BF16),
            pltpu.VMEM(flat, F32),
            pltpu.VMEM((1, planes), I32),
            pltpu.VMEM((rows, rows), BF16),
            pltpu.VMEM((rows, rows), BF16),
            pltpu.VMEM(modes.shape, F32),
            pltpu.VMEM(halves, BF16),
            pltpu.VMEM(halves, BF16),
            pltpu.VMEM(halves, F32),
            pltpu.VMEM(halves, F32),
            pltpu.VMEM(flat, F32),
            pltpu.VMEM((1, LANES), I32),
            pltpu.VMEM((1, LANES), I32),
            *[pltpu.VMEM((spaces, 2 * groups + 1, 1, LANES), I32)] * 4,
            pltpu.VMEM((cases, *short), I32),
            pltpu.VMEM((cases, *short), I32),
            pltpu.VMEM(short, I32),
            pltpu.SemaphoreType.DMA((8,)),
            pltpu.SemaphoreType.DMA((2,)),
            pltpu.SemaphoreType.DMA((5,)),
            pltpu.SemaphoreType.DMA((5,)),
        ],
        compiler_params=pltpu.CompilerParams(
            collective_id=0, has_side_effects=True, vmem_limit_bytes=LIMIT * 1024 * 1024
        ),
    )(
        *(pltpu.with_memory_space_constraint(x, pltpu.HBM) for x in (forcing.reshape(flat),
        viscosity.reshape(flat),
        measured.reshape(flat),
        correction.reshape(flat),
        wall_rows,
        jnp.asarray(high),
        jnp.asarray(low),
        jnp.asarray(modes))),
    )
    pressure, gradient = pl.pallas_call(
        functools.partial(spread, cells, planes),
        out_shape=(jax.ShapeDtypeStruct(flat, F32), jax.ShapeDtypeStruct(flat, F32)),
        in_specs=[anywhere, pl.BlockSpec(memory_space=pltpu.VMEM)],
        out_specs=(anywhere,) * 2,
        scratch_shapes=[pltpu.VMEM(flat, F32), pltpu.SemaphoreType.DMA((2,))],
        compiler_params=pltpu.CompilerParams(vmem_limit_bytes=LIMIT * 1024 * 1024),
    )(pressure, words)
    return pressure.reshape(forcing.shape), gradient.reshape(correction.shape)


def solution(mesh):
    return jax.shard_map(
        shards,
        mesh=mesh,
        in_specs=(
            P("case", "space", None, None),
            P("case", "space", None, None),
            P("case", "space", None, None),
            P("space", None, None),
            P("case", None),
        ),
        out_specs=(P("case", "space", None, None), P("space", None, None)),
        check_vma=False,
    )
```
